128 devices in a mesh: row: 16 (over y, z), col: 8 (over x, core).
Axes of the slice: x: 4, y: 4, z: 4, core: 2. Of those that a mesh axis runs over, the one named last changes fastest.
Arguments:
- covariance: float32 [2, 16, 512, 4, 8, 512], P(None, 'row', None, None, 'col'), as said below
- noise_var: float32 [2, 16, 512], P(None, 'row'), may hold values from 0.3 to 1.5
- observed: float32 [2, 16, 512, 1024], P(None, 'row', None, 'col'), may hold values from -6 to 6
- cloud_free: int32 [2, 16, 512, 1024], P(None, 'row', None, 'col'), may hold values 0 or 1
Outputs:
- factor: float32 [2, 16, 512, 4, 8, 512], P(None, 'row', None, None, 'col')
- reduced: float32 [2, 16, 512, 1024], P(None, 'row', None, 'col')
The draws below stay inside these ranges and needn't reach their ends.
Inputs may be any that keep to these rules, and one draw needn't show every extreme that they name: covariance is symmetric and v^T covariance v >= 0.25 v^T v for every vector v.
All inputs are finite; a program needn't handle non-finite values. No bound on the sum of `cloud_free` on one device may be relied on, other than what follows from the above.
Results may differ from the reference program's by a relative error of at most 0.00024.
Values sent between devices are 32-bit elements; how exact they have to be, the bound alone decides.
A program may use at most 128 MiB of HBM per device.

```python
import math
import jax
import jax.numpy as jnp
from jax import lax

N = 16384
P_SIZE = 512
PANELS = 2
LR = 2
LC = 4
S = 1024
N_ROW = 16


def draw_covariance(key, part):
    key = jax.random.fold_in(key, 7)
    feature_count = N // 16
    factors = jnp.clip(jax.random.normal(key, (N, feature_count), jnp.float32), -4.0, 4.0)
    product = jnp.dot(factors, factors.T, precision=lax.Precision.HIGHEST) * (4.0 / feature_count)
    product = 0.5 * (product + product.T)
    diagonal_index = jnp.arange(N, dtype=jnp.int32)
    product = product.at[diagonal_index, diagonal_index].add(0.25)
    return product.reshape(LR, N // (LR * P_SIZE), P_SIZE, LC, N // (LC * P_SIZE), P_SIZE)


def place_ends(result, key, low, high):
    longest = result.shape.index(max(result.shape))
    spots = []
    for shift in (0, 1):
        where = [jax.random.randint(jax.random.fold_in(key, axis), (), 0, length) for axis, length in enumerate(result.shape)]
        where[longest] = (where[longest] + shift) % result.shape[longest]
        spots.append(tuple(where))
    return result.at[spots[0]].set(low).at[spots[1]].set(high)


def block_scale(own_key, extent, cuts, least, high):
    loudness = 1.0
    for axis_at, shards_of in cuts:
        steps = jax.random.uniform(jax.random.fold_in(jax.random.fold_in(own_key, 6), axis_at), (shards_of,), jnp.float32, least / len(cuts), high / len(cuts))
        loudness = loudness * jnp.repeat(jnp.exp(steps), extent[axis_at] // shards_of).reshape((-1,) + (1,) * (len(extent) - 1 - axis_at))
    return loudness


def noise(rng, dims, deviation, limit, shards=(), held_as=jnp.bfloat16):
    result = jax.random.normal(rng, dims, jnp.float32) * deviation
    if len(shards) > 0:
        result = block_scale(rng, dims, shards, -0.22, 0.18) * result
    return jnp.clip(result, min=-limit, max=limit).astype(held_as)


def setup_inputs(seed: int = 0) -> dict:
    splits = jax.random.split(jax.random.key(seed), 5)
    covariance = draw_covariance(jax.random.fold_in(splits[4], 71), 0)
    noise_var = jnp.clip(jnp.exp(math.log(1.5) - 1.60943787 * jax.random.uniform(splits[1], (LR, N_ROW, P_SIZE), jnp.float32) ** block_scale(splits[1], (LR, N_ROW, P_SIZE), ((1, 16),), -0.2, 0.2)), 0.3, 1.5)
    observed = noise(splits[2], (LR, N_ROW, P_SIZE, S), 1.0, 6.0, ((1, 16), (3, 8)), jnp.float32)
    cloud_free = place_ends((jax.random.randint(splits[3], (LR, N_ROW, P_SIZE, S), 0, 4) < 3).astype(jnp.int32), jax.random.fold_in(splits[3], 1), 0, 1)
    return {"covariance": covariance, "noise_var": noise_var, "observed": observed, "cloud_free": cloud_free}


HIGHEST = lax.Precision.HIGHEST

def reference(covariance, noise_var, observed, cloud_free):
    matrix = covariance.reshape(N, N)
    diagonal_index = jnp.arange(N, dtype=jnp.int32)
    matrix = matrix.at[diagonal_index, diagonal_index].add(noise_var.reshape(N))
    targets = (observed * cloud_free.astype(jnp.float32)).reshape(N, -1)
    for section in range(PANELS):
        start_row = section * P_SIZE
        stop_row = start_row + P_SIZE
        corner = jnp.linalg.cholesky(matrix[start_row:stop_row, start_row:stop_row])
        lower_part = lax.linalg.triangular_solve(corner, matrix[stop_row:, start_row:stop_row], left_side=False, lower=True, transpose_a=True)
        matrix = matrix.at[stop_row:, stop_row:].add(-jnp.dot(lower_part, lower_part.T, precision=HIGHEST))
        column_block = jnp.concatenate([jnp.zeros((start_row, P_SIZE), jnp.float32), corner, lower_part], axis=0)
        matrix = matrix.at[:, start_row:stop_row].set(column_block)
        head_solve = lax.linalg.triangular_solve(corner, targets[start_row:stop_row], left_side=True, lower=True)
        targets = jnp.concatenate([targets[:start_row], head_solve, targets[stop_row:] - jnp.dot(lower_part, head_solve, precision=HIGHEST)], axis=0)
    matrix = matrix.at[:PANELS * P_SIZE, PANELS * P_SIZE:].set(0.0)
    return (matrix.reshape(covariance.shape), targets.reshape(observed.shape))
```

```python
import jax
import jax.numpy as jnp
from jax import lax
from jax.experimental import pallas as pl
from jax.experimental.pallas import tpu as pltpu
from jax.sharding import PartitionSpec as P

MESH = pl.DeviceIdType.MESH
HIGHEST = lax.Precision.HIGHEST
HIGH = lax.Precision.HIGH
PW = 512
NB = 2 * PW
BK = 128
CH = 32
GC = 128

TREES = (
    (1, 11, 9, 0, 0, 7, 1, 0, 0, 4, 1, 0, 0, 4, 9, 0),
    (2, 0, 0, 0, 7, 8, 8, 14, 3, 3, 2, 2, 0, 0, 0, 0),
    (4, 0, 6, 14, 0, 0, 6, 1, 0, 0, 4, 1, 0, 0, 4, 13),
    (8, 0, 0, 0, 0, 0, 0, 0, 12, 8, 8, 12, 13, 11, 2, 2),
)


def spread_kernel(hsrc, gsrc, H, G, K, hr, hs, kr, ks, gr, gs):
    width = hsrc.shape[1]
    row, col = lax.axis_index("row"), lax.axis_index("col")
    y, z, x, core = row // 4, row % 4, col // 2, col % 2
    where = [
        (y * 4 + (z + 1) % 4, col),
        (((y + 1) % 4) * 4 + z, col),
        (y * 4 + (z + 3) % 4, col),
        (((y + 3) % 4) * 4 + z, col),
        (row, ((x + 1) % 4) * 2 + core),
        (row, ((x + 3) % 4) * 2 + core),
        (row, x * 2 + 1 - core),
    ]
    barrier = pltpu.get_barrier_semaphore()
    for device in where:
        pl.semaphore_signal(barrier, inc=1, device_id=device, device_id_type=MESH)
    pl.semaphore_wait(barrier, len(where))

    masks = []
    for root in range(2):
        place = y * 4 + (z + 4 - root) % 4
        per = []
        for tree in TREES:
            m = jnp.int32(0)
            for at, bits in enumerate(tree):
                if bits:
                    m = jnp.where(place == at, bits, m)
            per.append(m)
        masks.append(per)

    def hslice(ref, root, part, c):
        rows = pl.ds(c * CH, CH)
        cols = pl.ds(0, PW) if part == 0 else pl.ds(PW, width - PW)
        return ref.at[rows, cols] if root is None else ref.at[root, rows, cols]

    def kslice(block, c):
        return K.at[block, pl.ds(c * CH, CH), :]

    def gslice(half, g):
        return G.at[half, pl.ds(g * GC, GC), :]

    def remote(ref, send, recv, device):
        return pltpu.make_async_remote_copy(
            src_ref=ref, dst_ref=ref, send_sem=send, recv_sem=recv, device_id=device, device_id_type=MESH
        )

    for root in range(2):

        @pl.when(row == root)
        def _():
            for part in range(2):
                for c in range(16):
                    pltpu.make_async_copy(
                        hslice(hsrc, None, part, c), hslice(H, root, part, c), hr.at[root, part, c]
                    ).start()

    for half in range(2):

        @pl.when(col == half)
        def _():
            for g in range(8):
                pltpu.make_async_copy(gsrc.at[pl.ds(g * GC, GC), :], gslice(half, g), gr.at[half, g]).start()

    ends = []

    def send(cond, ref, ssem, recv, device):
        copy = remote(ref, ssem, recv, device)

        @pl.when(cond)
        def _():
            copy.start()

        ends.append((cond, copy))

    def h_step(root, part, c):
        ref = hslice(H, root, part, c)
        recv = hr.at[root, part, c]
        remote(ref, hs.at[root, part, c, 0], recv, where[0]).wait_recv()
        tree = c % 4
        for d in range(4):
            if any(bits >> d & 1 for bits in TREES[tree]):
                cond = (masks[root][tree] >> d) & 1 == 1
                send(cond, ref, hs.at[root, part, c, d], recv, where[d])
        if part == 0:
            for owner_core in range(2):
                if root == 1 and owner_core == 0:
                    continue
                block = root + owner_core

                @pl.when(col == owner_core)
                def _():
                    pltpu.make_async_copy(ref, kslice(block, c), kr.at[block, c]).start()

    def k_step(block, c, sibling):
        carrier = core == min(block, 1)
        ref, recv = kslice(block, c), kr.at[block, c]
        copy = remote(ref, ks.at[block, c, 0], recv, where[6])
        if sibling:

            @pl.when(jnp.logical_not(carrier))
            def _():
                copy.wait_recv()

            return

        @pl.when(carrier)
        def _():
            copy.wait_recv()

        along(carrier, ref, ks.at[block, c], recv, c % 2)

    def along(carrier, ref, sems, recv, way):
        goes = (x != 3) if way == 0 else (x != 1)
        send(jnp.logical_and(carrier, goes), ref, sems.at[0], recv, where[4 + way])
        send(carrier, ref, sems.at[1], recv, where[6])

    def g_step(half, g, sibling):
        carrier = core == half
        ref, recv = gslice(half, g), gr.at[half, g]
        copy = remote(ref, gs.at[half, g, 0], recv, where[6])
        if sibling:

            @pl.when(jnp.logical_not(carrier))
            def _():
                copy.wait_recv()

            return

        @pl.when(carrier)
        def _():
            copy.wait_recv()

        along(carrier, ref, gs.at[half, g], recv, g % 2)

    for n in range(20):
        if n < 16:
            root, part, seq = n // 4 % 2, n // 8, n % 4
            for tree in range(4):
                h_step(root, part, seq * 4 + tree)
        if 1 <= n < 9:
            root, seq = (n - 1) // 4, (n - 1) % 4
            for tree in range(4):
                for block in ((0, 1) if root == 0 else (2,)):
                    k_step(block, seq * 4 + tree, False)
        if 4 <= n < 20 and n % 2 == 0:
            for half in range(2):
                g_step(half, (n - 4) // 2, False)
    for block in range(3):
        for c in range(16):
            k_step(block, c, True)
    for half in range(2):
        for g in range(8):
            g_step(half, g, True)
    for cond, copy in ends:

        @pl.when(cond)
        def _():
            copy.wait_send()


def spread(hsrc, gsrc):
    width = hsrc.shape[1]
    dma = pltpu.SemaphoreType.DMA
    return pl.pallas_call(
        spread_kernel,
        out_shape=(
            jax.ShapeDtypeStruct((2, PW, width), jnp.float32),
            jax.ShapeDtypeStruct((2, NB, PW), jnp.float32),
            jax.ShapeDtypeStruct((3, PW, PW), jnp.float32),
        ),
        in_specs=[pl.BlockSpec(memory_space=pl.ANY)] * 2,
        out_specs=[pl.BlockSpec(memory_space=pl.ANY)] * 3,
        scratch_shapes=[
            dma((2, 2, 16)),
            dma((2, 2, 16, 4)),
            dma((3, 16)),
            dma((3, 16, 2)),
            dma((2, 8)),
            dma((2, 8, 2)),
        ],
        compiler_params=pltpu.CompilerParams(collective_id=0, has_side_effects=True),
    )(hsrc, gsrc)


def dot(a, b, dims=((1,), (0,))):
    return lax.dot_general(a, b, (dims, ((), ())), precision=HIGHEST, preferred_element_type=jnp.float32)


def recip(d):
    r = pltpu.reciprocal(d, approx=True)
    return r * (2.0 - d * r)


def factor128(read):
    lane = lax.broadcasted_iota(jnp.int32, (8, BK), 1)
    sub = lax.broadcasted_iota(jnp.int32, (8, BK), 0)
    R = [read(p) for p in range(16)]
    Q = [jnp.where(lane == sub + 8 * p, 1.0, 0.0) for p in range(16)]
    splat = lambda v: jnp.broadcast_to(v, (8, BK))
    U, W = [], []
    for p in range(16):
        B = [splat(R[p][:, 8 * p + k : 8 * p + k + 1]) for k in range(8)]
        below = {i: [splat(R[i][:, 8 * p + k : 8 * p + k + 1]) for k in range(8)] for i in range(p + 1, 16)}
        Rp, Qp = R[p], Q[p]
        pivots = None
        for j in range(8):
            d = splat(B[j][j : j + 1, :])
            inv = recip(d)
            pivots = d if pivots is None else jnp.where(sub == j, d, pivots)
            coef = jnp.where(sub > j, B[j] * inv, 0.0)
            ur, qr = splat(Rp[j : j + 1, :]), splat(Qp[j : j + 1, :])
            lead = {k: splat(B[k][j : j + 1, :]) for k in range(j + 1, 8)}
            for i in range(p + 1, 16):
                ci = below[i][j] * inv
                for k in range(j + 1, 8):
                    below[i][k] = below[i][k] - ci * lead[k]
                R[i] = R[i] - ci * ur
                Q[i] = Q[i] - ci * qr
            if j < 7:
                for k in range(j + 1, 8):
                    B[k] = B[k] - coef * lead[k]
                Rp = Rp - coef * ur
                Qp = Qp - coef * qr
        scale = lax.rsqrt(pivots)
        U.append(jnp.where(lane >= sub + 8 * p, Rp * scale, 0.0))
        W.append(Qp * scale)
    return U, W


def corner_kernel(k_ref, w_ref, E, D):
    count = NB // BK
    E[0:PW, 0:PW] = k_ref[0]
    E[0:PW, PW:NB] = k_ref[1]
    E[PW:NB, PW:NB] = k_ref[2]
    E[PW:NB, 0:PW] = jnp.zeros((PW, PW), jnp.float32)

    def step(k, carry):
        r0 = pl.multiple_of(k * BK, BK)
        U, W = factor128(lambda p: E[pl.ds(r0 + 8 * p, 8), pl.ds(r0, BK)])
        for p in range(16):
            D[pl.ds(8 * p, 8), :] = W[p]
        E[pl.ds(r0, BK), :] = dot(D[...], E[pl.ds(r0, BK), :])
        E[pl.ds(r0, BK), pl.ds(r0, BK)] = D[...]
        lane = lax.broadcasted_iota(jnp.int32, (BK, NB), 1)
        w_ref[pl.ds(r0, BK), :] = jnp.where(lane < r0 + BK, E[pl.ds(r0, BK), :], 0.0)

        def under(i, carry):
            i0 = pl.multiple_of(i * BK, BK)
            E[pl.ds(i0, BK), pl.ds(r0, BK)] = jnp.zeros((BK, BK), jnp.float32)
            E[pl.ds(i0, BK), :] = E[pl.ds(i0, BK), :] - dot(
                E[pl.ds(r0, BK), pl.ds(i0, BK)], E[pl.ds(r0, BK), :], ((0,), (0,))
            )
            return carry

        lax.fori_loop(k + 1, count, under, 0)
        return carry

    lax.fori_loop(0, count, step, 0)


def corner(blocks):
    return pl.pallas_call(
        corner_kernel,
        out_shape=jax.ShapeDtypeStruct((NB, NB), jnp.float32),
        scratch_shapes=[pltpu.VMEM((NB, NB), jnp.float32), pltpu.VMEM((BK, BK), jnp.float32)],
        compiler_params=pltpu.CompilerParams(vmem_limit_bytes=40 * 2**20),
    )(blocks)


def body(covariance, noise_var, observed, cloud_free):
    row, col = lax.axis_index("row"), lax.axis_index("col")
    series = observed.shape[3]
    matrix = covariance.reshape(2, PW, 4, PW)
    noise = noise_var.reshape(2, PW)
    targets = (observed * cloud_free.astype(jnp.float32)).reshape(2, PW, series)
    rows = jnp.arange(2, dtype=jnp.int32) * 16 + row
    cols = jnp.arange(4, dtype=jnp.int32) * 8 + col
    same = (rows[:, None] == cols[None, :])[:, None, :, None]
    eye = jnp.eye(PW, dtype=bool)[None, :, None, :]
    matrix = matrix + jnp.where(jnp.logical_and(same, eye), noise[:, :, None, None], 0.0)
    wide = matrix.reshape(NB, 4 * PW)
    hsrc = jnp.concatenate([wide[:PW], targets[0]], axis=1)
    H, G, K = spread(hsrc, wide[:, :PW])
    W = corner(K)
    H = H.reshape(NB, 4 * PW + series)
    left = jnp.concatenate([G[0], G[1]], axis=1)
    X = lax.dot_general(left, W, (((1,), (1,)), ((), ())), precision=HIGH)
    T = jnp.dot(X, W, precision=HIGH)
    full = jnp.concatenate([wide, targets.reshape(NB, series)], axis=1) - jnp.dot(T, H, precision=HIGH)
    head = jnp.dot(W, H[:, 4 * PW :], precision=HIGH).reshape(2, PW, series)
    reduced = full[:, 4 * PW :].reshape(2, PW, series)
    head_here = jnp.where(row == 0, head[0], head[1])
    first = jnp.where(row < 2, head_here, reduced[0])
    reduced = jnp.stack([first, reduced[1]])
    panel = jnp.where(col == 0, X[:, :PW], X[:, PW:])
    r_at = (rows[:, None] * PW + jnp.arange(PW, dtype=jnp.int32)[None, :]).reshape(NB)
    c_at = col * PW + jnp.arange(PW, dtype=jnp.int32)
    panel = jnp.where(r_at[:, None] >= c_at[None, :], panel, 0.0)
    rest = jnp.where(r_at[:, None] < NB, 0.0, full[:, : 4 * PW])
    factor = jnp.concatenate([jnp.where(col < 2, panel, rest[:, :PW]), rest[:, PW:]], axis=1)
    return factor.reshape(covariance.shape), reduced.reshape(observed.shape)


def solution(mesh):
    placed = (
        P(None, "row", None, None, "col", None),
        P(None, "row", None),
        P(None, "row", None, "col"),
        P(None, "row", None, "col"),
    )
    return jax.shard_map(
        body,
        mesh=mesh,
        in_specs=placed,
        out_specs=(P(None, "row", None, None, "col", None), P(None, "row", None, "col")),
        check_vma=False,
    )
```

```python
import jax
import jax.numpy as jnp
from jax import lax
from jax.experimental import pallas as pl
from jax.experimental.pallas import tpu as pltpu
from jax.sharding import PartitionSpec as P

MESH = pl.DeviceIdType.MESH
HIGHEST = lax.Precision.HIGHEST
HIGH = lax.Precision.HIGH
PW = 512
NB = 2 * PW
BK = 128
CH = 32
GC = 64

TREES = (
    (1, 11, 9, 0, 0, 7, 1, 0, 0, 4, 1, 0, 0, 4, 9, 0),
    (2, 0, 0, 0, 7, 8, 8, 14, 3, 3, 2, 2, 0, 0, 0, 0),
    (4, 0, 6, 14, 0, 0, 6, 1, 0, 0, 4, 1, 0, 0, 4, 13),
    (8, 0, 0, 0, 0, 0, 0, 0, 12, 8, 8, 12, 13, 11, 2, 2),
)


def tree_table():
    step = ((0, 1), (1, 0), (0, -1), (-1, 0))
    table = []
    for tree in TREES:
        depth = {0: 0}
        stack = [0]
        while stack:
            at = stack.pop()
            for d in range(4):
                if tree[at] >> d & 1:
                    to = (at // 4 + step[d][0]) % 4 * 4 + (at % 4 + step[d][1]) % 4
                    depth[to] = depth[at] + 1
                    stack.append(to)
        table.append([tree[at] | depth[at] << 4 for at in range(16)])
    return table


class Spread:
    SLOTS = 23
    LATE = (0, 1)

    def __init__(self, hsrc, tsrc, gsrc, H, Tg, G, K, hr, hs, tr, ts, kr, ks, gr, gs):
        self.hsrc, self.tsrc, self.gsrc = hsrc, tsrc, gsrc
        self.H, self.Tg, self.G, self.K = H, Tg, G, K
        self.hr, self.hs, self.tr, self.ts = hr, hs, tr, ts
        self.kr, self.ks, self.gr, self.gs = kr, ks, gr, gs
        row, col = lax.axis_index("row"), lax.axis_index("col")
        y, z, x, core = row // 4, row % 4, col // 2, col % 2
        self.row, self.col, self.x, self.core = row, col, x, core
        self.where = [
            (y * 4 + (z + 1) % 4, col),
            (((y + 1) % 4) * 4 + z, col),
            (y * 4 + (z + 3) % 4, col),
            (((y + 3) % 4) * 4 + z, col),
            (row, ((x + 1) % 4) * 2 + core),
            (row, ((x + 3) % 4) * 2 + core),
            (row, x * 2 + 1 - core),
        ]
        self.mask, self.depth = [], []
        for root in range(2):
            place = y * 4 + (z + 4 - root) % 4
            masks, depths = [], []
            for entries in tree_table():
                v = jnp.int32(0)
                for at, entry in enumerate(entries):
                    v = jnp.where(place == at, entry, v)
                masks.append(v & 15)
                depths.append((v >> 4) + self.LATE[root])
            self.mask.append(masks)
            self.depth.append(depths)
        self.hops = [x, (4 - x) % 4]
        self.on = [x != 3, x != 1]

    def remote(self, src, dst, send, recv, to):
        return pltpu.make_async_remote_copy(
            src_ref=src, dst_ref=dst, send_sem=send, recv_sem=recv, device_id=self.where[to], device_id_type=MESH
        )

    def hpiece(self, root, tree, n):
        at = pl.multiple_of((n % 4) * BK + tree * CH, CH)
        return self.H.at[root, pl.ds(at, CH), pl.ds(pl.multiple_of((n // 4) * PW, PW), PW)]

    def hsrc_piece(self, tree, n):
        at = pl.multiple_of((n % 4) * BK + tree * CH, CH)
        return self.hsrc.at[pl.ds(at, CH), pl.ds(pl.multiple_of((n // 4) * PW, PW), PW)]

    def kpiece(self, block, tree, n):
        return self.K.at[block, pl.ds(pl.multiple_of(n * BK + tree * CH, CH), CH), :]

    def gpiece(self, half, g):
        return self.G.at[half, pl.ds(pl.multiple_of(g * GC, GC), GC), :]

    def start(self):
        barrier = pltpu.get_barrier_semaphore()
        for device in self.where:
            pl.semaphore_signal(barrier, inc=1, device_id=device, device_id_type=MESH)
        for root in range(2):

            @pl.when(self.row == root)
            def _():
                def own(n, carry):
                    for tree in range(4):
                        pltpu.make_async_copy(
                            self.hsrc_piece(tree, n), self.hpiece(root, tree, n), self.hr.at[root, tree, n]
                        ).start()
                    return carry

                lax.fori_loop(0, 16, own, 0)
                for tree in range(4):
                    rows = pl.ds(tree * BK, BK)
                    pltpu.make_async_copy(
                        self.tsrc.at[rows, :], self.Tg.at[root, rows, :], self.tr.at[root, tree]
                    ).start()

        for half in range(2):

            @pl.when(self.col == half)
            def _():
                def own(g, carry):
                    rows = pl.ds(pl.multiple_of(g * GC, GC), GC)
                    pltpu.make_async_copy(self.gsrc.at[rows, :], self.gpiece(half, g), self.gr.at[half, g]).start()
                    return carry

                lax.fori_loop(0, 16, own, 0)
        pl.semaphore_wait(barrier, len(self.where))

    def slot(self, s):
        for root in range(2):
            for tree in range(4):
                self.h_slot(root, tree, s - self.depth[root][tree])
        for block in range(3):
            for tree in range(4):
                root, way = block // 2, tree % 2
                n = s - self.depth[root][tree] - self.hops[way]
                here = jnp.logical_and(self.core == min(block, 1), self.x != 0)

                @pl.when(jnp.logical_and(here, jnp.logical_and(n >= 0, n < 4)))
                def _():
                    piece, recv = self.kpiece(block, tree, n), self.kr.at[block, tree, n]
                    self.remote(piece, piece, self.ks.at[block, tree, 0], recv, 6).wait_recv()

                    @pl.when(self.on[way])
                    def _():
                        self.remote(piece, piece, self.ks.at[block, tree, 0], recv, 4 + way).start()

                    self.remote(piece, piece, self.ks.at[block, tree, 1], recv, 6).start()

        for half in range(2):
            for way in range(2):
                t = s - 3 - self.hops[way]
                g = (t // 2) * 2 + way
                valid = jnp.logical_and(jnp.logical_and(t >= 0, t < 16), t % 2 == 0)

                @pl.when(jnp.logical_and(valid, self.core == half))
                def _():
                    piece, recv = self.gpiece(half, g), self.gr.at[half, g]
                    self.remote(piece, piece, self.gs.at[half, way, 0], recv, 6).wait_recv()

                    @pl.when(self.on[way])
                    def _():
                        self.remote(piece, piece, self.gs.at[half, way, 0], recv, 4 + way).start()

                    self.remote(piece, piece, self.gs.at[half, way, 1], recv, 6).start()

    def dirs(self, tree):
        return [d for d in range(4) if any(bits >> d & 1 for bits in TREES[tree])]

    def has(self, root, tree, d):
        return (self.mask[root][tree] >> d) & 1 == 1

    def h_slot(self, root, tree, n):
        @pl.when(jnp.logical_and(n >= 0, n < 16))
        def _():
            piece, recv = self.hpiece(root, tree, n), self.hr.at[root, tree, n]
            self.remote(piece, piece, self.hs.at[root, tree, 0], recv, 0).wait_recv()
            for d in self.dirs(tree):

                @pl.when(self.has(root, tree, d))
                def _():
                    self.remote(piece, piece, self.hs.at[root, tree, d], recv, d).start()

            for core in range(2):
                block = root + core
                if (root, core) == (1, 0):
                    continue

                @pl.when(jnp.logical_and(self.col == core, n < 4))
                def _():
                    m = jnp.minimum(n, 3)
                    to, krecv = self.kpiece(block, tree, m), self.kr.at[block, tree, m]
                    pltpu.make_async_copy(piece, to, krecv).start()
                    self.remote(piece, to, self.ks.at[block, tree, 0], krecv, 4 + tree % 2).start()
                    self.remote(piece, to, self.ks.at[block, tree, 1], krecv, 6).start()

        @pl.when(n == 16)
        def _():
            piece, recv = self.Tg.at[root, pl.ds(tree * BK, BK), :], self.tr.at[root, tree]
            self.remote(piece, piece, self.ts.at[root, tree, 0], recv, 0).wait_recv()
            for d in self.dirs(tree):

                @pl.when(self.has(root, tree, d))
                def _():
                    self.remote(piece, piece, self.ts.at[root, tree, d], recv, d).start()

    def corner_rows(self, block, n):
        @pl.when(jnp.logical_or(self.core != min(block, 1), self.x == 0))
        def _():
            for tree in range(4):
                piece, recv = self.kpiece(block, tree, n), self.kr.at[block, tree, n]
                self.remote(piece, piece, self.ks.at[block, tree, 0], recv, 6).wait_recv()

    def finish(self):
        for half in range(2):

            @pl.when(self.core != half)
            def _():
                def one(g, carry):
                    piece, recv = self.gpiece(half, g), self.gr.at[half, g]
                    self.remote(piece, piece, self.gs.at[half, 0, 0], recv, 6).wait_recv()
                    return carry

                lax.fori_loop(0, 16, one, 0)

            @pl.when(self.core == half)
            def _():
                for way in range(2):
                    whole = self.G.at[half, pl.ds(0, PW), :]
                    wait_sent(self, whole, self.gs.at[half, way, 1])

                    @pl.when(self.on[way])
                    def _():
                        wait_sent(self, whole, self.gs.at[half, way, 0])

        for root in range(2):
            for tree in range(4):
                for d in self.dirs(tree):

                    @pl.when(self.has(root, tree, d))
                    def _():
                        wait_sent(self, self.H.at[root, :, pl.ds(0, PW)], self.hs.at[root, tree, d])
                        wait_sent(self, self.Tg.at[root, pl.ds(tree * BK, BK), :], self.ts.at[root, tree, d])

        for block in range(3):

            @pl.when(self.core == min(block, 1))
            def _():
                for tree in range(4):
                    whole = self.K.at[block, pl.ds(0, BK), :]
                    wait_sent(self, whole, self.ks.at[block, tree, 1])

                    @pl.when(self.on[tree % 2])
                    def _():
                        wait_sent(self, whole, self.ks.at[block, tree, 0])


def wait_sent(spread, whole, sem):
    spread.remote(whole, whole, sem, spread.gr.at[0, 0], 6).wait_send()


def spread_semaphores():
    dma = pltpu.SemaphoreType.DMA
    return [
        dma((2, 4, 16)),
        dma((2, 4, 4)),
        dma((2, 4)),
        dma((2, 4, 4)),
        dma((3, 4, 4)),
        dma((3, 4, 2)),
        dma((2, 16)),
        dma((2, 2, 2)),
    ]


def dot(a, b, dims=((1,), (0,))):
    return lax.dot_general(a, b, (dims, ((), ())), precision=HIGHEST, preferred_element_type=jnp.float32)


def recip(d):
    r = pltpu.reciprocal(d, approx=True)
    return r * (2.0 - d * r)


def factor128(read):
    lane = lax.broadcasted_iota(jnp.int32, (8, BK), 1)
    sub = lax.broadcasted_iota(jnp.int32, (8, BK), 0)
    R = [read(p) for p in range(16)]
    Q = [jnp.where(lane == sub + 8 * p, 1.0, 0.0) for p in range(16)]
    splat = lambda v: jnp.broadcast_to(v, (8, BK))
    W = []
    for p in range(16):
        B = [splat(R[p][:, 8 * p + k : 8 * p + k + 1]) for k in range(8)]
        below = {i: [splat(R[i][:, 8 * p + k : 8 * p + k + 1]) for k in range(8)] for i in range(p + 1, 16)}
        Rp, Qp = R[p], Q[p]
        pivots = None
        for j in range(8):
            d = splat(B[j][j : j + 1, :])
            inv = recip(d)
            pivots = d if pivots is None else jnp.where(sub == j, d, pivots)
            coef = jnp.where(sub > j, B[j] * inv, 0.0)
            ur, qr = splat(Rp[j : j + 1, :]), splat(Qp[j : j + 1, :])
            lead = {k: splat(B[k][j : j + 1, :]) for k in range(j + 1, 8)}
            for i in range(p + 1, 16):
                ci = below[i][j] * inv
                for k in range(j + 1, 8):
                    below[i][k] = below[i][k] - ci * lead[k]
                R[i] = R[i] - ci * ur
                Q[i] = Q[i] - ci * qr
            if j < 7:
                for k in range(j + 1, 8):
                    B[k] = B[k] - coef * lead[k]
                Rp = Rp - coef * ur
                Qp = Qp - coef * qr
        scale = lax.rsqrt(pivots)
        W.append(Qp * scale)
    return W


def split(v):
    hi = v.astype(jnp.bfloat16)
    return hi, (v - hi.astype(jnp.float32)).astype(jnp.bfloat16)


def dot3(a, b, dims=((1,), (0,))):
    one = lambda u, v: lax.dot_general(u, v, (dims, ((), ())), preferred_element_type=jnp.float32)
    return one(a[0], b[0]) + (one(a[0], b[1]) + one(a[1], b[0]))


PRE = 9
PER = 2


def front_kernel(hsrc, tsrc, gsrc, t_out, x_out, h_out, g_out, head_out, H, Tg, G, K, E, D, Gh, Gl, Wh, Wl, out_sem, *sems):
    spread = Spread(hsrc, tsrc, gsrc, H, Tg, G, K, *sems)
    count = NB // BK

    def slots(first, n):
        def one(s, carry):
            spread.slot(s)
            return carry

        lax.fori_loop(first, first + n, one, 0)

    spread.start()
    E[...] = jnp.zeros_like(E)
    slots(0, PRE)
    lane = lax.broadcasted_iota(jnp.int32, (BK, NB), 1)

    def step(k, carry):
        r0 = pl.multiple_of(k * BK, BK)
        rows = pl.ds(r0, BK)
        spread.slot(PRE + PER * k)

        @pl.when(k < 4)
        def _():
            n = jnp.minimum(k, 3)
            spread.corner_rows(0, n)
            spread.corner_rows(1, n)
            at = pl.ds(pl.multiple_of(n * BK, BK), BK)
            E[rows, 0:PW] = E[rows, 0:PW] + jnp.where(lane[:, :PW] >= r0, K[0, at, :], 0.0)
            E[rows, PW:NB] = E[rows, PW:NB] + K[1, at, :]

        @pl.when(k >= 4)
        def _():
            n = jnp.maximum(k - 4, 0)
            spread.corner_rows(2, n)
            at = pl.ds(pl.multiple_of(n * BK, BK), BK)
            E[rows, PW:NB] = E[rows, PW:NB] + jnp.where(lane[:, PW:] >= r0, K[2, at, :], 0.0)

        W = factor128(lambda p: E[pl.ds(r0 + 8 * p, 8), pl.ds(r0, BK)])
        for p in range(16):
            D[pl.ds(8 * p, 8), :] = W[p]
        spread.slot(PRE + PER * k + 1)
        E[rows, :] = dot(D[...], E[rows, :])
        E[rows, pl.ds(r0, BK)] = D[...]
        hi, lo = split(jnp.where(lane < r0 + BK, E[rows, :], 0.0))
        Wh[rows, :] = hi
        Wl[rows, :] = lo

        def under(i, carry):
            i0 = pl.multiple_of(i * BK, BK)
            E[pl.ds(i0, BK), pl.ds(r0, BK)] = jnp.zeros((BK, BK), jnp.float32)
            E[pl.ds(i0, BK), :] = E[pl.ds(i0, BK), :] - dot(E[rows, pl.ds(i0, BK)], E[rows, :], ((0,), (0,)))
            return carry

        lax.fori_loop(k + 1, count, under, 0)
        return carry

    lax.fori_loop(0, count, step, 0)
    spread.finish()
    outs = [pltpu.make_async_copy(H, h_out, out_sem.at[0]), pltpu.make_async_copy(Tg, g_out, out_sem.at[1])]
    for copy in outs:
        copy.start()

    q = PW // 2

    def block(i, carry):
        rows = pl.ds(pl.multiple_of(i * q, q), q)
        gh, gl = [], []
        for half in range(2):
            hi, lo = split(G[half, rows, :])
            Gh[:, half * PW : (half + 1) * PW] = hi
            Gl[:, half * PW : (half + 1) * PW] = lo
        for j in range(4):
            to = pl.ds(j * q, q)
            kk = pl.ds(0, (j + 1) * q)
            E[rows, to] = dot3((Gh[:, kk], Gl[:, kk]), (Wh[to, kk], Wl[to, kk]), ((1,), (1,)))
        hi, lo = split(E[rows, :])
        Gh[...] = hi
        Gl[...] = lo
        for j in range(4):
            kk = pl.ds(j * q, NB - j * q)
            to = pl.ds(j * q, q)
            G[j // 2, rows, pl.ds(j % 2 * q, q)] = dot3((Gh[:, kk], Gl[:, kk]), (Wh[kk, to], Wl[kk, to]))
        return carry

    lax.fori_loop(0, 4, block, 0)
    outs.append(pltpu.make_async_copy(G, t_out, out_sem.at[2]))
    outs[2].start()
    outs.append(pltpu.make_async_copy(E.at[:, pl.ds(pl.multiple_of(spread.core * PW, PW), PW)], x_out, out_sem.at[3]))
    outs[3].start()
    for half in range(2):
        kh = [split(Tg[part]) for part in range(half + 1)]
        total = jnp.zeros((PW, BK), jnp.float32)
        for part in range(half + 1):
            kk = pl.ds(part * PW, PW)
            to = pl.ds(half * PW, PW)
            total = total + dot3((Wh[to, kk], Wl[to, kk]), kh[part])
        K[half, :, 0:BK] = total
    outs.append(pltpu.make_async_copy(K.at[pl.ds(0, 2), :, pl.ds(0, BK)], head_out, out_sem.at[4]))
    outs[4].start()
    for copy in outs:
        copy.wait()


def front(hsrc, tsrc, gsrc):
    f32, bf16 = jnp.float32, jnp.bfloat16
    series = tsrc.shape[1]
    return pl.pallas_call(
        front_kernel,
        out_shape=(
            jax.ShapeDtypeStruct((2, NB, PW), f32),
            jax.ShapeDtypeStruct((NB, PW), f32),
            jax.ShapeDtypeStruct((2, PW, 4 * PW), f32),
            jax.ShapeDtypeStruct((2, PW, series), f32),
            jax.ShapeDtypeStruct((2, PW, series), f32),
        ),
        in_specs=[pl.BlockSpec(memory_space=pl.ANY)] * 3,
        out_specs=[pl.BlockSpec(memory_space=pl.ANY)] * 5,
        scratch_shapes=[
            pltpu.VMEM((2, PW, 4 * PW), f32),
            pltpu.VMEM((2, PW, series), f32),
            pltpu.VMEM((2, NB, PW), f32),
            pltpu.VMEM((3, PW, PW), f32),
            pltpu.VMEM((NB, NB), f32),
            pltpu.VMEM((BK, BK), f32),
            pltpu.VMEM((PW // 2, NB), bf16),
            pltpu.VMEM((PW // 2, NB), bf16),
            pltpu.VMEM((NB, NB), bf16),
            pltpu.VMEM((NB, NB), bf16),
            pltpu.SemaphoreType.DMA((5,)),
        ]
        + spread_semaphores(),
        compiler_params=pltpu.CompilerParams(collective_id=0, has_side_effects=True, vmem_limit_bytes=56 * 2**20),
    )(hsrc, tsrc, gsrc)


def diagonal(block, noise, c, s):
    row, col = lax.axis_index("row"), lax.axis_index("col")
    size = noise.shape[0]
    a, first = block // (PW // size), block % (PW // size) * size
    i = lax.broadcasted_iota(jnp.int32, (size, BK), 0) + first
    j = lax.broadcasted_iota(jnp.int32, (size, BK), 1) + s * BK
    on = a * 16 + row == c * 8 + col
    return jnp.where(jnp.logical_and(i == j, on), noise, 0.0)


def prepare_kernel(cov, noise, hsrc, gsrc):
    block = pl.program_id(0)
    for s in range(16):
        tile = cov[:, s, :]
        if s < 4:
            tile = tile + diagonal(block, noise[...], 0, s)
            gsrc[:, s * BK : (s + 1) * BK] = tile

        @pl.when(block < 4)
        def _():
            hsrc[:, s * BK : (s + 1) * BK] = tile


def prepare(cov, noise):
    return pl.pallas_call(
        prepare_kernel,
        grid=(8,),
        out_shape=(jax.ShapeDtypeStruct((PW, 4 * PW), jnp.float32), jax.ShapeDtypeStruct((NB, PW), jnp.float32)),
        in_specs=[pl.BlockSpec((BK, 16, BK), lambda i: (i, 0, 0)), pl.BlockSpec((BK, 1), lambda i: (i, 0))],
        out_specs=[
            pl.BlockSpec((BK, 4 * PW), lambda i: (jnp.minimum(i, 3), 0)),
            pl.BlockSpec((BK, PW), lambda i: (i, 0)),
        ],
        compiler_params=pltpu.CompilerParams(vmem_limit_bytes=32 * 2**20),
    )(cov, noise)


UR = 256


def update_kernel(cov, noise, T, H, Tg, X, targets, head, out, reduced, Hh, Hl, Sh, Sl):
    step = pl.program_id(0)
    row, col = lax.axis_index("row"), lax.axis_index("col")

    @pl.when(step == 0)
    def _():
        def one(i, carry):
            rows = pl.ds(pl.multiple_of(i * BK, BK), BK)
            Hh[rows, :], Hl[rows, :] = split(H[rows, :])
            Sh[rows, :], Sl[rows, :] = split(Tg[rows, :])
            return carry

        lax.fori_loop(0, NB // BK, one, 0)

    lead = jnp.logical_and(row < 2, step < PW // UR)
    t0, t1 = split(T[0]), split(T[1])

    def minus(hi, lo, c0, n):
        to = pl.ds(c0, n)
        top, low = pl.ds(0, PW), pl.ds(PW, PW)
        return dot3(t0, (hi[top, to], lo[top, to])) + dot3(t1, (hi[low, to], lo[low, to]))

    i = lax.broadcasted_iota(jnp.int32, (UR, BK), 0) + (step // (PW // UR) * 16 + row) * PW + step % (PW // UR) * UR
    for b in range(8):
        d = minus(Hh, Hl, b * 256, 256)
        for e in range(2):
            s = 2 * b + e
            value = cov[:, s, :] + diagonal(step, noise[...], s // 4, s % 4) - d[:, e * BK : (e + 1) * BK]
            value = jnp.where(lead, 0.0, value)
            if s < 4:
                j = lax.broadcasted_iota(jnp.int32, (UR, BK), 1) + col * PW + s * BK
                value = jnp.where(col < 2, jnp.where(i >= j, X[:, s * BK : (s + 1) * BK], 0.0), value)
            out[:, s, :] = value
    reduced[...] = jnp.where(lead, head[...], targets[...] - minus(Sh, Sl, 0, BK))


def update(cov, noise, T, H, Tg, X, targets, head):
    series = targets.shape[1]
    whole = lambda shape: pl.BlockSpec(shape, lambda i: (0,) * len(shape))
    rows = lambda n: pl.BlockSpec((UR, n), lambda i: (i, 0))
    bf16 = jnp.bfloat16
    return pl.pallas_call(
        update_kernel,
        grid=(NB // UR,),
        out_shape=(jax.ShapeDtypeStruct(cov.shape, jnp.float32), jax.ShapeDtypeStruct(targets.shape, jnp.float32)),
        in_specs=[
            pl.BlockSpec((UR, 16, BK), lambda i: (i, 0, 0)),
            rows(1),
            pl.BlockSpec((2, UR, PW), lambda i: (0, i, 0)),
            whole((NB, 4 * PW)),
            whole((NB, series)),
            rows(PW),
            rows(series),
            pl.BlockSpec((UR, series), lambda i: (i % (PW // UR), 0)),
        ],
        out_specs=[pl.BlockSpec((UR, 16, BK), lambda i: (i, 0, 0)), rows(series)],
        scratch_shapes=[
            pltpu.VMEM((NB, 4 * PW), bf16),
            pltpu.VMEM((NB, 4 * PW), bf16),
            pltpu.VMEM((NB, series), bf16),
            pltpu.VMEM((NB, series), bf16),
        ],
        compiler_params=pltpu.CompilerParams(vmem_limit_bytes=56 * 2**20),
    )(cov, noise, T, H, Tg, X, targets, head)


def body(covariance, noise_var, observed, cloud_free):
    row = lax.axis_index("row")
    series = observed.shape[3]
    cov = covariance.reshape(NB, 16, BK)
    noise = noise_var.reshape(NB, 1)
    targets = (observed * cloud_free.astype(jnp.float32)).reshape(NB, series)
    hsrc, gsrc = prepare(cov, noise)
    T, X, H, Tg, head = front(hsrc, targets[:PW], gsrc)
    head = jnp.where(row == 0, head[0], head[1])
    factor, reduced = update(cov, noise, T, H.reshape(NB, 4 * PW), Tg.reshape(NB, series), X, targets, head)
    return factor.reshape(covariance.shape), reduced.reshape(observed.shape)


def solution(mesh):
    placed = (
        P(None, "row", None, None, "col", None),
        P(None, "row", None),
        P(None, "row", None, "col"),
        P(None, "row", None, "col"),
    )
    return jax.shard_map(
        body,
        mesh=mesh,
        in_specs=placed,
        out_specs=(P(None, "row", None, None, "col", None), P(None, "row", None, "col")),
        check_vma=False,
    )
```

```python
import jax
import jax.numpy as jnp
from jax import lax
from jax.experimental import pallas as pl
from jax.experimental.pallas import tpu as pltpu
from jax.sharding import PartitionSpec as P

MESH = pl.DeviceIdType.MESH
HIGHEST = lax.Precision.HIGHEST
HIGH = lax.Precision.HIGH
PW = 512
NB = 2 * PW
BK = 128
CH = 32
GC = 64

TREES = (
    (1, 11, 9, 0, 0, 7, 1, 0, 0, 4, 1, 0, 0, 4, 9, 0),
    (2, 0, 0, 0, 7, 8, 8, 14, 3, 3, 2, 2, 0, 0, 0, 0),
    (4, 0, 6, 14, 0, 0, 6, 1, 0, 0, 4, 1, 0, 0, 4, 13),
    (8, 0, 0, 0, 0, 0, 0, 0, 12, 8, 8, 12, 13, 11, 2, 2),
)


def tree_table():
    step = ((0, 1), (1, 0), (0, -1), (-1, 0))
    table = []
    for tree in TREES:
        depth = {0: 0}
        stack = [0]
        while stack:
            at = stack.pop()
            for d in range(4):
                if tree[at] >> d & 1:
                    to = (at // 4 + step[d][0]) % 4 * 4 + (at % 4 + step[d][1]) % 4
                    depth[to] = depth[at] + 1
                    stack.append(to)
        table.append([tree[at] | depth[at] << 4 for at in range(16)])
    return table


class Spread:
    LATE = (0, 4)
    GLATE = 9

    def __init__(self, cov, noise, tsrc, H, Tg, G, K, own, hr, hs, tr, ts, kr, ks, gr, gs):
        self.cov, self.noise, self.tsrc, self.own = cov, noise, tsrc, own
        self.H, self.Tg, self.G, self.K = H, Tg, G, K
        self.hr, self.hs, self.tr, self.ts = hr, hs, tr, ts
        self.kr, self.ks, self.gr, self.gs = kr, ks, gr, gs
        row, col = lax.axis_index("row"), lax.axis_index("col")
        y, z, x, core = row // 4, row % 4, col // 2, col % 2
        self.row, self.col, self.x, self.core = row, col, x, core
        self.where = [
            (y * 4 + (z + 1) % 4, col),
            (((y + 1) % 4) * 4 + z, col),
            (y * 4 + (z + 3) % 4, col),
            (((y + 3) % 4) * 4 + z, col),
            (row, ((x + 1) % 4) * 2 + core),
            (row, ((x + 3) % 4) * 2 + core),
            (row, x * 2 + 1 - core),
        ]
        self.mask, self.depth = [], []
        for root in range(2):
            place = y * 4 + (z + 4 - root) % 4
            masks, depths = [], []
            for entries in tree_table():
                v = jnp.int32(0)
                for at, entry in enumerate(entries):
                    v = jnp.where(place == at, entry, v)
                masks.append(v & 15)
                depths.append(v >> 4)
            self.mask.append(masks)
            self.depth.append(depths)
        self.hops = [x, (4 - x) % 4]
        self.on = [x != 3, x != 1]

    def remote(self, src, dst, send, recv, to):
        return pltpu.make_async_remote_copy(
            src_ref=src, dst_ref=dst, send_sem=send, recv_sem=recv, device_id=self.where[to], device_id_type=MESH
        )

    def hpiece(self, root, tree, n):
        at = pl.multiple_of((n % 4) * BK + tree * CH, CH)
        return self.H.at[root, pl.ds(at, CH), n // 4]

    def kpiece(self, block, tree, n):
        return self.K.at[block, pl.ds(pl.multiple_of(n * BK + tree * CH, CH), CH)]

    def gpiece(self, half, g):
        return self.G.at[half, g // 8, pl.ds(pl.multiple_of(g % 8 * GC, GC), GC)]

    def start(self):
        barrier = pltpu.get_barrier_semaphore()
        for device in self.where:
            pl.semaphore_signal(barrier, inc=1, device_id=device, device_id_type=MESH)
        for root in range(2):
            corner = pltpu.make_async_copy(self.cov.at[0, :, 0], self.H.at[root, :, 0], self.own)

            @pl.when(self.row == root)
            def _():
                corner.start()

                def own(n, carry):
                    for tree in range(4):
                        at = pl.multiple_of((n % 4) * BK + tree * CH, CH)
                        pltpu.make_async_copy(
                            self.cov.at[0, pl.ds(at, CH), n // 4],
                            self.hpiece(root, tree, n),
                            self.hr.at[root, tree, n],
                        ).start()
                    return carry

                lax.fori_loop(4, 16, own, 0)
                for tree in range(4):
                    rows = pl.ds(tree * BK, BK)
                    pltpu.make_async_copy(
                        self.tsrc.at[rows, :], self.Tg.at[root, rows, :], self.tr.at[root, tree]
                    ).start()
                corner.wait()

            @pl.when(jnp.logical_and(self.row == root, self.col == root))
            def _():
                for s in range(4):
                    rows = pl.ds(s * BK, BK)
                    self.H[root, rows, 0, s, :] = self.H[root, rows, 0, s, :] + on_diagonal(self.noise[s : s + 1, :])

        for half in range(2):

            @pl.when(self.col == half)
            def _():
                def own(g, carry):
                    pltpu.make_async_copy(
                        self.cov.at[g // 8, pl.ds(pl.multiple_of(g % 8 * GC, GC), GC), 0],
                        self.gpiece(half, g),
                        self.gr.at[half, g],
                    ).start()
                    return carry

                lax.fori_loop(0, 16, own, 0)
        pl.semaphore_wait(barrier, len(self.where))

    def slot(self, s):
        for root in range(2):
            for tree in range(4):
                depth, late = self.depth[root][tree], s - self.LATE[root]
                self.h_slot(root, tree, jnp.where(late - depth < 4, late - depth, jnp.where(late - 2 * depth < 4, -1, late - 2 * depth)))
        for block in range(3):
            for tree in range(4):
                root, way = block // 2, tree % 2
                n = s - self.LATE[root] - self.depth[root][tree] - self.hops[way]
                here = jnp.logical_and(self.core == min(block, 1), self.x != 0)

                @pl.when(jnp.logical_and(here, jnp.logical_and(n >= 0, n < 4)))
                def _():
                    piece, recv = self.kpiece(block, tree, n), self.kr.at[block, tree, n]
                    self.remote(piece, piece, self.ks.at[block, tree, 0], recv, 6).wait_recv()

                    @pl.when(self.on[way])
                    def _():
                        self.remote(piece, piece, self.ks.at[block, tree, 0], recv, 4 + way).start()

                    self.remote(piece, piece, self.ks.at[block, tree, 1], recv, 6).start()

        for half in range(2):
            for way in range(2):
                t = s - self.GLATE - 2 * self.hops[way]
                g = (t // 2) * 2 + way
                valid = jnp.logical_and(jnp.logical_and(t >= 0, t < 16), t % 2 == 0)

                @pl.when(jnp.logical_and(valid, self.core == half))
                def _():
                    piece, recv = self.gpiece(half, g), self.gr.at[half, g]
                    self.remote(piece, piece, self.gs.at[half, way, 0], recv, 6).wait_recv()

                    @pl.when(self.on[way])
                    def _():
                        self.remote(piece, piece, self.gs.at[half, way, 0], recv, 4 + way).start()

                    self.remote(piece, piece, self.gs.at[half, way, 1], recv, 6).start()

    def dirs(self, tree):
        return [d for d in range(4) if any(bits >> d & 1 for bits in TREES[tree])]

    def has(self, root, tree, d):
        return (self.mask[root][tree] >> d) & 1 == 1

    def h_slot(self, root, tree, n):
        @pl.when(jnp.logical_and(n >= 0, n < 16))
        def _():
            piece, recv = self.hpiece(root, tree, n), self.hr.at[root, tree, n]

            @pl.when(jnp.logical_or(self.row != root, n >= 4))
            def _():
                self.remote(piece, piece, self.hs.at[root, tree, 0], recv, 0).wait_recv()

            for d in self.dirs(tree):

                @pl.when(self.has(root, tree, d))
                def _():
                    self.remote(piece, piece, self.hs.at[root, tree, d], recv, d).start()

            for core in range(2):
                block = root + core
                if (root, core) == (1, 0):
                    continue

                @pl.when(jnp.logical_and(self.col == core, n < 4))
                def _():
                    m = jnp.minimum(n, 3)
                    to, krecv = self.kpiece(block, tree, m), self.kr.at[block, tree, m]
                    pltpu.make_async_copy(piece, to, krecv).start()
                    self.remote(piece, to, self.ks.at[block, tree, 0], krecv, 4 + tree % 2).start()
                    self.remote(piece, to, self.ks.at[block, tree, 1], krecv, 6).start()

        @pl.when(n == 16)
        def _():
            piece, recv = self.Tg.at[root, pl.ds(tree * BK, BK), :], self.tr.at[root, tree]
            self.remote(piece, piece, self.ts.at[root, tree, 0], recv, 0).wait_recv()
            for d in self.dirs(tree):

                @pl.when(self.has(root, tree, d))
                def _():
                    self.remote(piece, piece, self.ts.at[root, tree, d], recv, d).start()

    def corner_rows(self, block, n):
        @pl.when(jnp.logical_or(self.core != min(block, 1), self.x == 0))
        def _():
            for tree in range(4):
                piece, recv = self.kpiece(block, tree, n), self.kr.at[block, tree, n]
                self.remote(piece, piece, self.ks.at[block, tree, 0], recv, 6).wait_recv()

    def finish(self):
        for half in range(2):

            @pl.when(self.core != half)
            def _():
                def one(g, carry):
                    piece, recv = self.gpiece(half, g), self.gr.at[half, g]
                    self.remote(piece, piece, self.gs.at[half, 0, 0], recv, 6).wait_recv()
                    return carry

                lax.fori_loop(0, 16, one, 0)

            @pl.when(self.core == half)
            def _():
                for way in range(2):
                    whole = self.G.at[half, 0]
                    wait_sent(self, whole, self.gs.at[half, way, 1])

                    @pl.when(self.on[way])
                    def _():
                        wait_sent(self, whole, self.gs.at[half, way, 0])

        for root in range(2):
            for tree in range(4):
                for d in self.dirs(tree):

                    @pl.when(self.has(root, tree, d))
                    def _():
                        wait_sent(self, self.H.at[root, :, 0], self.hs.at[root, tree, d])
                        wait_sent(self, self.Tg.at[root, pl.ds(tree * BK, BK), :], self.ts.at[root, tree, d])

        for block in range(3):

            @pl.when(self.core == min(block, 1))
            def _():
                for tree in range(4):
                    whole = self.K.at[block, pl.ds(0, BK)]
                    wait_sent(self, whole, self.ks.at[block, tree, 1])

                    @pl.when(self.on[tree % 2])
                    def _():
                        wait_sent(self, whole, self.ks.at[block, tree, 0])


def on_diagonal(line):
    i = lax.broadcasted_iota(jnp.int32, (BK, BK), 0)
    j = lax.broadcasted_iota(jnp.int32, (BK, BK), 1)
    return jnp.where(i == j, line, 0.0)


def wait_sent(spread, whole, sem):
    spread.remote(whole, whole, sem, spread.gr.at[0, 0], 6).wait_send()


def spread_semaphores():
    dma = pltpu.SemaphoreType.DMA
    return [
        dma,
        dma((2, 4, 16)),
        dma((2, 4, 4)),
        dma((2, 4)),
        dma((2, 4, 4)),
        dma((3, 4, 4)),
        dma((3, 4, 2)),
        dma((2, 16)),
        dma((2, 2, 2)),
    ]


def dot(a, b, dims=((1,), (0,))):
    return lax.dot_general(a, b, (dims, ((), ())), precision=HIGHEST, preferred_element_type=jnp.float32)


def recip(d):
    r = pltpu.reciprocal(d, approx=True)
    return r * (2.0 - d * r)


def factor128(read, halfway):
    lane = lax.broadcasted_iota(jnp.int32, (8, BK), 1)
    sub = lax.broadcasted_iota(jnp.int32, (8, BK), 0)
    R = [read(p) for p in range(16)]
    Q = [jnp.where(lane == sub + 8 * p, 1.0, 0.0) for p in range(16)]
    splat = lambda v: jnp.broadcast_to(v, (8, BK))
    W = []
    for p in range(16):
        if p == 8:
            halfway()
        B = [splat(R[p][:, 8 * p + k : 8 * p + k + 1]) for k in range(8)]
        below = {i: [splat(R[i][:, 8 * p + k : 8 * p + k + 1]) for k in range(8)] for i in range(p + 1, 16)}
        Rp, Qp = R[p], Q[p]
        pivots = None
        for j in range(8):
            d = splat(B[j][j : j + 1, :])
            inv = recip(d)
            pivots = d if pivots is None else jnp.where(sub == j, d, pivots)
            coef = jnp.where(sub > j, B[j] * inv, 0.0)
            ur, qr = splat(Rp[j : j + 1, :]), splat(Qp[j : j + 1, :])
            lead = {k: splat(B[k][j : j + 1, :]) for k in range(j + 1, 8)}
            for i in range(p + 1, 16):
                ci = below[i][j] * inv
                for k in range(j + 1, 8):
                    below[i][k] = below[i][k] - ci * lead[k]
                R[i] = R[i] - ci * ur
                Q[i] = Q[i] - ci * qr
            if j < 7:
                for k in range(j + 1, 8):
                    B[k] = B[k] - coef * lead[k]
                Rp = Rp - coef * ur
                Qp = Qp - coef * qr
        scale = lax.rsqrt(pivots)
        W.append(Qp * scale)
    return W


def split(v):
    hi = v.astype(jnp.bfloat16)
    return hi, (v - hi.astype(jnp.float32)).astype(jnp.bfloat16)


def dot3(a, b, dims=((1,), (0,))):
    one = lambda u, v: lax.dot_general(u, v, (dims, ((), ())), preferred_element_type=jnp.float32)
    return one(a[0], b[0]) + (one(a[0], b[1]) + one(a[1], b[0]))


PRE = 9
PER = 3


def front_kernel(cov, noise, tsrc, t_out, x_out, h_out, g_out, head_out, H, Tg, G, K, E, T, D, Gh, Gl, Wh, Wl, Hd, out_sem, *sems):
    spread = Spread(cov, noise, tsrc, H, Tg, G, K, *sems)
    count = NB // BK

    def slots(first, n):
        def one(s, carry):
            spread.slot(s)
            return carry

        lax.fori_loop(first, first + n, one, 0)

    K2, G2 = K.reshape(3 * PW * 4, BK), G.reshape(2 * NB * 4, BK)
    spread.start()
    E[...] = jnp.zeros_like(E)
    slots(0, PRE)
    lane = lax.broadcasted_iota(jnp.int32, (BK, NB), 1)

    def step(k, carry):
        r0 = pl.multiple_of(k * BK, BK)
        rows = pl.ds(r0, BK)
        spread.slot(PRE + PER * k)

        @pl.when(k < 4)
        def _():
            n = jnp.minimum(k, 3)
            spread.corner_rows(0, n)
            spread.corner_rows(1, n)
            for s in range(4):
                to = slice(s * BK, (s + 1) * BK)
                E[rows, to] = E[rows, to] + jnp.where(lane[:, to] >= r0, K2[pl.ds(n * (BK * 4) + s, BK, stride=4), :], 0.0)
            for s in range(4):
                to = slice(PW + s * BK, PW + (s + 1) * BK)
                E[rows, to] = E[rows, to] + K2[pl.ds((PW + n * BK) * 4 + s, BK, stride=4), :]

        @pl.when(k >= 4)
        def _():
            n = jnp.maximum(k - 4, 0)
            spread.corner_rows(2, n)
            for s in range(4):
                to = slice(PW + s * BK, PW + (s + 1) * BK)
                E[rows, to] = E[rows, to] + jnp.where(lane[:, to] >= r0, K2[pl.ds((2 * PW + n * BK) * 4 + s, BK, stride=4), :], 0.0)

        W = factor128(lambda p: E[pl.ds(r0 + 8 * p, 8), pl.ds(r0, BK)], lambda: spread.slot(PRE + PER * k + 1))
        for p in range(16):
            D[pl.ds(8 * p, 8), :] = W[p]
        spread.slot(PRE + PER * k + 2)
        E[rows, :] = dot(D[...], E[rows, :])
        E[rows, pl.ds(r0, BK)] = D[...]
        hi, lo = split(jnp.where(lane < r0 + BK, E[rows, :], 0.0))
        Wh[rows, :] = hi
        Wl[rows, :] = lo

        def under(i, carry):
            i0 = pl.multiple_of(i * BK, BK)
            E[pl.ds(i0, BK), pl.ds(r0, BK)] = jnp.zeros((BK, BK), jnp.float32)
            E[pl.ds(i0, BK), :] = E[pl.ds(i0, BK), :] - dot(E[rows, pl.ds(i0, BK)], E[rows, :], ((0,), (0,)))
            return carry

        lax.fori_loop(k + 1, count, under, 0)
        return carry

    lax.fori_loop(0, count, step, 0)
    spread.finish()
    outs = [pltpu.make_async_copy(H, h_out, out_sem.at[0]), pltpu.make_async_copy(Tg, g_out, out_sem.at[1])]
    for copy in outs:
        copy.start()

    q = PW // 2

    def block(i, carry):
        rows = pl.ds(pl.multiple_of(i * q, q), q)
        gh, gl = [], []
        mine = jnp.logical_and(spread.row == spread.col, i < 2)
        for half in range(2):
            for s in range(4):
                for e in range(2):
                    value = G2[pl.ds((half * NB + i * q + e * BK) * 4 + s, BK, stride=4), :]
                    here = jnp.logical_and(jnp.logical_and(mine, spread.row == half), i % 2 * 2 + e == s)
                    value = value + jnp.where(here, on_diagonal(noise[s : s + 1, :]), 0.0)
                    hi, lo = split(value)
                    to = slice(half * PW + s * BK, half * PW + (s + 1) * BK)
                    Gh[e * BK : (e + 1) * BK, to] = hi
                    Gl[e * BK : (e + 1) * BK, to] = lo
        for j in range(4):
            to = pl.ds(j * q, q)
            kk = pl.ds(0, (j + 1) * q)
            E[rows, to] = dot3((Gh[:, kk], Gl[:, kk]), (Wh[to, kk], Wl[to, kk]), ((1,), (1,)))
        hi, lo = split(E[rows, :])
        Gh[...] = hi
        Gl[...] = lo
        for j in range(4):
            kk = pl.ds(j * q, NB - j * q)
            to = pl.ds(j * q, q)
            T[rows, to] = dot3((Gh[:, kk], Gl[:, kk]), (Wh[kk, to], Wl[kk, to]))
        return carry

    lax.fori_loop(0, 4, block, 0)
    outs.append(pltpu.make_async_copy(T, t_out, out_sem.at[2]))
    outs[2].start()
    outs.append(pltpu.make_async_copy(E.at[:, pl.ds(pl.multiple_of(spread.core * PW, PW), PW)], x_out, out_sem.at[3]))
    outs[3].start()
    for half in range(2):
        kh = [split(Tg[part]) for part in range(half + 1)]
        total = jnp.zeros((PW, BK), jnp.float32)
        for part in range(half + 1):
            kk = pl.ds(part * PW, PW)
            to = pl.ds(half * PW, PW)
            total = total + dot3((Wh[to, kk], Wl[to, kk]), kh[part])
        Hd[half] = total
    outs.append(pltpu.make_async_copy(Hd, head_out, out_sem.at[4]))
    outs[4].start()
    for copy in outs:
        copy.wait()


def front(cov, noise, tsrc):
    f32, bf16 = jnp.float32, jnp.bfloat16
    series = tsrc.shape[1]
    return pl.pallas_call(
        front_kernel,
        out_shape=(
            jax.ShapeDtypeStruct((NB, NB), f32),
            jax.ShapeDtypeStruct((NB, PW), f32),
            jax.ShapeDtypeStruct((2, PW, 4, 4, BK), f32),
            jax.ShapeDtypeStruct((2, PW, series), f32),
            jax.ShapeDtypeStruct((2, PW, series), f32),
        ),
        in_specs=[
            pl.BlockSpec(memory_space=pl.ANY),
            pl.BlockSpec(memory_space=pltpu.VMEM),
            pl.BlockSpec(memory_space=pl.ANY),
        ],
        out_specs=[pl.BlockSpec(memory_space=pl.ANY)] * 5,
        scratch_shapes=[
            pltpu.VMEM((2, PW, 4, 4, BK), f32),
            pltpu.VMEM((2, PW, series), f32),
            pltpu.VMEM((2, 2, PW, 4, BK), f32),
            pltpu.VMEM((3, PW, 4, BK), f32),
            pltpu.VMEM((NB, NB), f32),
            pltpu.VMEM((NB, NB), f32),
            pltpu.VMEM((BK, BK), f32),
            pltpu.VMEM((PW // 2, NB), bf16),
            pltpu.VMEM((PW // 2, NB), bf16),
            pltpu.VMEM((NB, NB), bf16),
            pltpu.VMEM((NB, NB), bf16),
            pltpu.VMEM((2, PW, series), f32),
            pltpu.SemaphoreType.DMA((5,)),
        ]
        + spread_semaphores(),
        compiler_params=pltpu.CompilerParams(collective_id=0, has_side_effects=True, vmem_limit_bytes=56 * 2**20),
    )(cov, noise, tsrc)


UR = 256


def update_kernel(cov, noise, T, H, Tg, X, targets, head, out, reduced, Hh, Hl, Sh, Sl):
    step = pl.program_id(0)
    row, col = lax.axis_index("row"), lax.axis_index("col")

    @pl.when(step == 0)
    def _():
        def one(i, carry):
            rows = pl.ds(pl.multiple_of(i * BK, BK), BK)
            for s in range(16):
                to = slice(s * BK, (s + 1) * BK)
                Hh[rows, to], Hl[rows, to] = split(H[pl.ds(i * (BK * 16) + s, BK, stride=16), :])
            Sh[rows, :], Sl[rows, :] = split(Tg[rows, :])
            return carry

        lax.fori_loop(0, NB // BK, one, 0)

    lead = jnp.logical_and(row < 2, step < PW // UR)
    t0, t1 = split(T[:, 0:PW]), split(T[:, PW:NB])

    def minus(hi, lo, c0, n):
        to = pl.ds(c0, n)
        top, low = pl.ds(0, PW), pl.ds(PW, PW)
        return dot3(t0, (hi[top, to], lo[top, to])) + dot3(t1, (hi[low, to], lo[low, to]))

    i = lax.broadcasted_iota(jnp.int32, (UR, BK), 0) + (step // (PW // UR) * 16 + row) * PW + step % (PW // UR) * UR
    shifted = lax.broadcasted_iota(jnp.int32, (UR, BK), 0) - lax.broadcasted_iota(jnp.int32, (UR, BK), 1)
    for b in range(8):
        d = minus(Hh, Hl, b * 256, 256)
        for e in range(2):
            s = 2 * b + e
            on = jnp.logical_and(step // 2 * 16 + row == s // 4 * 8 + col, step % 2 == s % 4 // 2)
            line = jnp.where(on, noise[pl.ds(step // 2 * 4 + s % 4, 1), :], 0.0)
            value = cov[pl.ds(s, UR, stride=16), :] + jnp.where(shifted == s % 2 * BK, line, 0.0) - d[:, e * BK : (e + 1) * BK]
            value = jnp.where(lead, 0.0, value)
            if s < 4:
                j = lax.broadcasted_iota(jnp.int32, (UR, BK), 1) + col * PW + s * BK
                value = jnp.where(col < 2, jnp.where(i >= j, X[:, s * BK : (s + 1) * BK], 0.0), value)
            out[pl.ds(s, UR, stride=16), :] = value
    reduced[...] = jnp.where(lead, jnp.where(row == 0, head[0], head[1]), targets[...] - minus(Sh, Sl, 0, BK))


def update(cov, noise, T, H, Tg, X, targets, head):
    series = targets.shape[1]
    whole = lambda shape: pl.BlockSpec(shape, lambda i: (0,) * len(shape))
    rows = lambda n, m=1: pl.BlockSpec((UR * m, n), lambda i: (i, 0))
    bf16 = jnp.bfloat16
    return pl.pallas_call(
        update_kernel,
        grid=(NB // UR,),
        out_shape=(jax.ShapeDtypeStruct(cov.shape, jnp.float32), jax.ShapeDtypeStruct(targets.shape, jnp.float32)),
        in_specs=[
            rows(BK, 16),
            whole((8, BK)),
            rows(NB),
            whole((NB * 16, BK)),
            whole((NB, series)),
            rows(PW),
            rows(series),
            pl.BlockSpec((2, UR, series), lambda i: (0, i % (PW // UR), 0)),
        ],
        out_specs=[rows(BK, 16), rows(series)],
        scratch_shapes=[
            pltpu.VMEM((NB, 4 * PW), bf16),
            pltpu.VMEM((NB, 4 * PW), bf16),
            pltpu.VMEM((NB, series), bf16),
            pltpu.VMEM((NB, series), bf16),
        ],
        compiler_params=pltpu.CompilerParams(vmem_limit_bytes=56 * 2**20),
    )(cov, noise, T, H, Tg, X, targets, head)


def body(covariance, noise_var, observed, cloud_free):
    series = observed.shape[3]
    noise = noise_var.reshape(8, BK)
    targets = (observed * cloud_free.astype(jnp.float32)).reshape(NB, series)
    T, X, H, Tg, head = front(covariance.reshape(2, PW, 4, 4, BK), noise, targets[:PW])
    factor, reduced = update(
        covariance.reshape(NB * 16, BK), noise, T, H.reshape(NB * 16, BK), Tg.reshape(NB, series), X, targets, head
    )
    return factor.reshape(covariance.shape), reduced.reshape(observed.shape)


def solution(mesh):
    placed = (
        P(None, "row", None, None, "col", None),
        P(None, "row", None),
        P(None, "row", None, "col"),
        P(None, "row", None, "col"),
    )
    return jax.shard_map(
        body,
        mesh=mesh,
        in_specs=placed,
        out_specs=(P(None, "row", None, None, "col", None), P(None, "row", None, "col")),
        check_vma=False,
    )
```

```python
import jax
import jax.numpy as jnp
from jax import lax
from jax.experimental import pallas as pl
from jax.experimental.pallas import tpu as pltpu
from jax.sharding import PartitionSpec as P

MESH = pl.DeviceIdType.MESH
PW = 512
NB = 2 * PW
BK = 128
CH = 32
GC = 64

TREES = (
    (1, 11, 9, 0, 0, 7, 1, 0, 0, 4, 1, 0, 0, 4, 9, 0),
    (2, 0, 0, 0, 7, 8, 8, 14, 3, 3, 2, 2, 0, 0, 0, 0),
    (4, 0, 6, 14, 0, 0, 6, 1, 0, 0, 4, 1, 0, 0, 4, 13),
    (8, 0, 0, 0, 0, 0, 0, 0, 12, 8, 8, 12, 13, 11, 2, 2),
)


def tree_table():
    step = ((0, 1), (1, 0), (0, -1), (-1, 0))
    table = []
    for tree in TREES:
        depth = {0: 0}
        stack = [0]
        while stack:
            at = stack.pop()
            for d in range(4):
                if tree[at] >> d & 1:
                    to = (at // 4 + step[d][0]) % 4 * 4 + (at % 4 + step[d][1]) % 4
                    depth[to] = depth[at] + 1
                    stack.append(to)
        table.append([tree[at] | depth[at] << 4 for at in range(16)])
    return table


class Spread:
    LATE = (0, 4)
    GLATE = 9

    def __init__(self, cov, noise, tsrc, H, Tg, G, K, own, hr, hs, tr, ts, kr, ks, gr, gs):
        self.cov, self.noise, self.tsrc, self.own = cov, noise, tsrc, own
        self.H, self.Tg, self.G, self.K = H, Tg, G, K
        self.hr, self.hs, self.tr, self.ts = hr, hs, tr, ts
        self.kr, self.ks, self.gr, self.gs = kr, ks, gr, gs
        row, col = lax.axis_index("row"), lax.axis_index("col")
        y, z, x, core = row // 4, row % 4, col // 2, col % 2
        self.row, self.col, self.x, self.core = row, col, x, core
        self.where = [
            (y * 4 + (z + 1) % 4, col),
            (((y + 1) % 4) * 4 + z, col),
            (y * 4 + (z + 3) % 4, col),
            (((y + 3) % 4) * 4 + z, col),
            (row, ((x + 1) % 4) * 2 + core),
            (row, ((x + 3) % 4) * 2 + core),
            (row, x * 2 + 1 - core),
        ]
        self.mask, self.depth = [], []
        for root in range(2):
            place = y * 4 + (z + 4 - root) % 4
            masks, depths = [], []
            for entries in tree_table():
                v = jnp.int32(0)
                for at, entry in enumerate(entries):
                    v = jnp.where(place == at, entry, v)
                masks.append(v & 15)
                depths.append(v >> 4)
            self.mask.append(masks)
            self.depth.append(depths)
        self.hops = [x, (4 - x) % 4]
        self.on = [x != 3, x != 1]

    def remote(self, src, dst, send, recv, to):
        return pltpu.make_async_remote_copy(
            src_ref=src, dst_ref=dst, send_sem=send, recv_sem=recv, device_id=self.where[to], device_id_type=MESH
        )

    def hpiece(self, root, tree, n):
        at = pl.multiple_of((n % 4) * BK + tree * CH, CH)
        return self.H.at[root, pl.ds(at, CH), n // 4]

    def kpiece(self, block, tree, n):
        return self.K.at[block, pl.ds(pl.multiple_of(n * BK + tree * CH, CH), CH)]

    def gpiece(self, half, g):
        return self.G.at[half, g // 8, pl.ds(pl.multiple_of(g % 8 * GC, GC), GC)]

    def start(self):
        barrier = pltpu.get_barrier_semaphore()
        for device in self.where:
            pl.semaphore_signal(barrier, inc=1, device_id=device, device_id_type=MESH)
        for root in range(2):
            corner = pltpu.make_async_copy(self.cov.at[0, :, 0], self.H.at[root, :, 0], self.own)

            @pl.when(self.row == root)
            def _():
                corner.start()

                def own(n, carry):
                    for tree in range(4):
                        at = pl.multiple_of((n % 4) * BK + tree * CH, CH)
                        pltpu.make_async_copy(
                            self.cov.at[0, pl.ds(at, CH), n // 4],
                            self.hpiece(root, tree, n),
                            self.hr.at[root, tree, n],
                        ).start()
                    return carry

                lax.fori_loop(4, 16, own, 0)
                for tree in range(4):
                    rows = pl.ds(tree * BK, BK)
                    pltpu.make_async_copy(
                        self.tsrc.at[rows, :], self.Tg.at[root, rows, :], self.tr.at[root, tree]
                    ).start()
                corner.wait()

            @pl.when(jnp.logical_and(self.row == root, self.col == root))
            def _():
                for s in range(4):
                    rows = pl.ds(s * BK, BK)
                    self.H[root, rows, 0, s, :] = self.H[root, rows, 0, s, :] + on_diagonal(self.noise[s : s + 1, :])

        for half in range(2):

            @pl.when(self.col == half)
            def _():
                def own(g, carry):
                    pltpu.make_async_copy(
                        self.cov.at[g // 8, pl.ds(pl.multiple_of(g % 8 * GC, GC), GC), 0],
                        self.gpiece(half, g),
                        self.gr.at[half, g],
                    ).start()
                    return carry

                lax.fori_loop(0, 16, own, 0)
        pl.semaphore_wait(barrier, len(self.where))

    def slot(self, s):
        for root in range(2):
            for tree in range(4):
                depth, late = self.depth[root][tree], s - self.LATE[root]
                self.h_slot(root, tree, jnp.where(late - depth < 4, late - depth, jnp.where(late - 2 * depth < 4, -1, late - 2 * depth)))
        for block in range(3):
            for tree in range(4):
                root, way = block // 2, tree % 2
                n = s - self.LATE[root] - self.depth[root][tree] - self.hops[way]
                here = jnp.logical_and(self.core == min(block, 1), self.x != 0)

                @pl.when(jnp.logical_and(here, jnp.logical_and(n >= 0, n < 4)))
                def _():
                    piece, recv = self.kpiece(block, tree, n), self.kr.at[block, tree, n]
                    self.remote(piece, piece, self.ks.at[block, tree, 0], recv, 6).wait_recv()

                    @pl.when(self.on[way])
                    def _():
                        self.remote(piece, piece, self.ks.at[block, tree, 0], recv, 4 + way).start()

                    self.remote(piece, piece, self.ks.at[block, tree, 1], recv, 6).start()

        for half in range(2):
            for way in range(2):
                t = s - self.GLATE - 2 * self.hops[way]
                g = (t // 2) * 2 + way
                valid = jnp.logical_and(jnp.logical_and(t >= 0, t < 16), t % 2 == 0)

                @pl.when(jnp.logical_and(valid, self.core == half))
                def _():
                    piece, recv = self.gpiece(half, g), self.gr.at[half, g]
                    self.remote(piece, piece, self.gs.at[half, way, 0], recv, 6).wait_recv()

                    @pl.when(self.on[way])
                    def _():
                        self.remote(piece, piece, self.gs.at[half, way, 0], recv, 4 + way).start()

                    self.remote(piece, piece, self.gs.at[half, way, 1], recv, 6).start()

    def dirs(self, tree):
        return [d for d in range(4) if any(bits >> d & 1 for bits in TREES[tree])]

    def has(self, root, tree, d):
        return (self.mask[root][tree] >> d) & 1 == 1

    def h_slot(self, root, tree, n):
        @pl.when(jnp.logical_and(n >= 0, n < 16))
        def _():
            piece, recv = self.hpiece(root, tree, n), self.hr.at[root, tree, n]

            @pl.when(jnp.logical_or(self.row != root, n >= 4))
            def _():
                self.remote(piece, piece, self.hs.at[root, tree, 0], recv, 0).wait_recv()

            for d in self.dirs(tree):

                @pl.when(self.has(root, tree, d))
                def _():
                    self.remote(piece, piece, self.hs.at[root, tree, d], recv, d).start()

            for core in range(2):
                block = root + core
                if (root, core) == (1, 0):
                    continue

                @pl.when(jnp.logical_and(self.col == core, n < 4))
                def _():
                    m = jnp.minimum(n, 3)
                    to, krecv = self.kpiece(block, tree, m), self.kr.at[block, tree, m]
                    pltpu.make_async_copy(piece, to, krecv).start()
                    self.remote(piece, to, self.ks.at[block, tree, 0], krecv, 4 + tree % 2).start()
                    self.remote(piece, to, self.ks.at[block, tree, 1], krecv, 6).start()

        @pl.when(n == 16)
        def _():
            piece, recv = self.Tg.at[root, pl.ds(tree * BK, BK), :], self.tr.at[root, tree]
            self.remote(piece, piece, self.ts.at[root, tree, 0], recv, 0).wait_recv()
            for d in self.dirs(tree):

                @pl.when(self.has(root, tree, d))
                def _():
                    self.remote(piece, piece, self.ts.at[root, tree, d], recv, d).start()

    def corner_rows(self, block, n):
        @pl.when(jnp.logical_or(self.core != min(block, 1), self.x == 0))
        def _():
            for tree in range(4):
                piece, recv = self.kpiece(block, tree, n), self.kr.at[block, tree, n]
                self.remote(piece, piece, self.ks.at[block, tree, 0], recv, 6).wait_recv()

    def finish(self):
        for half in range(2):

            @pl.when(self.core != half)
            def _():
                def one(g, carry):
                    piece, recv = self.gpiece(half, g), self.gr.at[half, g]
                    self.remote(piece, piece, self.gs.at[half, 0, 0], recv, 6).wait_recv()
                    return carry

                lax.fori_loop(0, 16, one, 0)

            @pl.when(self.core == half)
            def _():
                for way in range(2):
                    whole = self.G.at[half, 0]
                    wait_sent(self, whole, self.gs.at[half, way, 1])

                    @pl.when(self.on[way])
                    def _():
                        wait_sent(self, whole, self.gs.at[half, way, 0])

        for root in range(2):
            for tree in range(4):
                for d in self.dirs(tree):

                    @pl.when(self.has(root, tree, d))
                    def _():
                        wait_sent(self, self.H.at[root, :, 0], self.hs.at[root, tree, d])
                        wait_sent(self, self.Tg.at[root, pl.ds(tree * BK, BK), :], self.ts.at[root, tree, d])

        for block in range(3):

            @pl.when(self.core == min(block, 1))
            def _():
                for tree in range(4):
                    whole = self.K.at[block, pl.ds(0, BK)]
                    wait_sent(self, whole, self.ks.at[block, tree, 1])

                    @pl.when(self.on[tree % 2])
                    def _():
                        wait_sent(self, whole, self.ks.at[block, tree, 0])


def on_diagonal(line):
    i = lax.broadcasted_iota(jnp.int32, (BK, BK), 0)
    j = lax.broadcasted_iota(jnp.int32, (BK, BK), 1)
    return jnp.where(i == j, line, 0.0)


def wait_sent(spread, whole, sem):
    spread.remote(whole, whole, sem, spread.gr.at[0, 0], 6).wait_send()


def spread_semaphores():
    dma = pltpu.SemaphoreType.DMA
    return [
        dma,
        dma((2, 4, 16)),
        dma((2, 4, 4)),
        dma((2, 4)),
        dma((2, 4, 4)),
        dma((3, 4, 4)),
        dma((3, 4, 2)),
        dma((2, 16)),
        dma((2, 2, 2)),
    ]


def factor128(read, halfway):
    lane = lax.broadcasted_iota(jnp.int32, (8, BK), 1)
    sub = lax.broadcasted_iota(jnp.int32, (8, BK), 0)
    R = [read(p) for p in range(16)]
    Q = [jnp.where(lane == sub + 8 * p, 1.0, 0.0) for p in range(16)]
    splat = lambda v: jnp.broadcast_to(v, (8, BK))
    W = []
    for p in range(16):
        if p == 8:
            halfway()
        B = [splat(R[p][:, 8 * p + k : 8 * p + k + 1]) for k in range(8)]
        below = {i: [splat(R[i][:, 8 * p + k : 8 * p + k + 1]) for k in range(8)] for i in range(p + 1, 16)}
        Rp, Qp = R[p], Q[p]
        pivots = None
        for j in range(8):
            d = splat(B[j][j : j + 1, :])
            inv = pltpu.reciprocal(d, approx=True)
            pivots = d if pivots is None else jnp.where(sub == j, d, pivots)
            coef = jnp.where(sub > j, B[j] * inv, 0.0)
            ur, qr = splat(Rp[j : j + 1, :]), splat(Qp[j : j + 1, :])
            lead = {k: splat(B[k][j : j + 1, :]) for k in range(j + 1, 8)}
            for i in range(p + 1, 16):
                ci = below[i][j] * inv
                for k in range(j + 1, 8):
                    below[i][k] = below[i][k] - ci * lead[k]
                R[i] = R[i] - ci * ur
                Q[i] = Q[i] - ci * qr
            if j < 7:
                for k in range(j + 1, 8):
                    B[k] = B[k] - coef * lead[k]
                Rp = Rp - coef * ur
                Qp = Qp - coef * qr
        scale = lax.rsqrt(pivots)
        W.append(Qp * scale)
    return W


def split(v):
    hi = v.astype(jnp.bfloat16)
    return hi, (v - hi.astype(jnp.float32)).astype(jnp.bfloat16)


def dot3(a, b, dims=((1,), (0,))):
    one = lambda u, v: lax.dot_general(u, v, (dims, ((), ())), preferred_element_type=jnp.float32)
    return one(a[0], b[0]) + (one(a[0], b[1]) + one(a[1], b[0]))


def less_above(k, line, Uh, Ul, Wh, Wl):
    for c in range(1, NB // BK):

        @pl.when(k == c)
        def _():
            top, here = pl.ds(0, c * BK), pl.ds(c * BK, BK)
            u = (Uh[top, here], Ul[top, here])
            for first in range(0, NB, 2 * BK):
                for hi, lo, start, stop in ((Wh, Wl, 0, c * BK), (Uh, Ul, c * BK, NB)):
                    start, stop = max(first, start), min(first + 2 * BK, stop)
                    if start < stop:
                        to = pl.ds(start, stop - start)
                        line[:, to] = line[:, to] - dot3(u, (hi[top, to], lo[top, to]), ((0,), (0,)))


def finish_row(r0, inverse, line, Uh, Ul, Wh, Wl):
    rows = pl.ds(r0, BK)
    whole = dot3(split(inverse[...]), split(line[...]))
    lane = lax.broadcasted_iota(jnp.int32, (BK, NB), 1)
    Uh[rows, :], Ul[rows, :] = split(jnp.where(lane >= r0 + BK, whole, 0.0))
    Wh[rows, :], Wl[rows, :] = split(jnp.where(lane < r0, whole, 0.0))
    Wh[rows, pl.ds(r0, BK)], Wl[rows, pl.ds(r0, BK)] = split(inverse[...])


PRE = 9
PER = 3


def front_kernel(cov, noise, tsrc, t_out, x_out, h_out, g_out, head_out, H, Tg, G, K, E, T, D, line, Uh, Ul, Gh, Gl, Wh, Wl, Hd, out_sem, *sems):
    spread = Spread(cov, noise, tsrc, H, Tg, G, K, *sems)
    count = NB // BK

    def slots(first, n):
        def one(s, carry):
            spread.slot(s)
            return carry

        lax.fori_loop(first, first + n, one, 0)

    K2, G2 = K.reshape(3 * PW * 4, BK), G.reshape(2 * NB * 4, BK)
    spread.start()
    slots(0, PRE)
    lane = lax.broadcasted_iota(jnp.int32, (BK, BK), 1)

    def step(k, carry):
        r0 = pl.multiple_of(k * BK, BK)
        spread.slot(PRE + PER * k)

        @pl.when(k < 4)
        def _():
            n = jnp.minimum(k, 3)
            spread.corner_rows(0, n)
            spread.corner_rows(1, n)
            for s in range(4):
                value = K2[pl.ds(n * (BK * 4) + s, BK, stride=4), :]
                line[:, s * BK : (s + 1) * BK] = jnp.where(lane + s * BK >= r0, value, 0.0)
                line[:, PW + s * BK : PW + (s + 1) * BK] = K2[pl.ds((PW + n * BK) * 4 + s, BK, stride=4), :]

        @pl.when(k >= 4)
        def _():
            n = jnp.maximum(k - 4, 0)
            spread.corner_rows(2, n)
            for s in range(4):
                value = K2[pl.ds((2 * PW + n * BK) * 4 + s, BK, stride=4), :]
                line[:, s * BK : (s + 1) * BK] = jnp.zeros((BK, BK), jnp.float32)
                line[:, PW + s * BK : PW + (s + 1) * BK] = jnp.where(lane + PW + s * BK >= r0, value, 0.0)

        less_above(k, line, Uh, Ul, Wh, Wl)
        W = factor128(lambda p: line[8 * p : 8 * p + 8, pl.ds(r0, BK)], lambda: spread.slot(PRE + PER * k + 1))
        for p in range(16):
            D[pl.ds(8 * p, 8), :] = W[p]
        spread.slot(PRE + PER * k + 2)
        finish_row(r0, D, line, Uh, Ul, Wh, Wl)
        return carry

    lax.fori_loop(0, count, step, 0)
    spread.finish()
    outs = [pltpu.make_async_copy(H, h_out, out_sem.at[0]), pltpu.make_async_copy(Tg, g_out, out_sem.at[1])]
    for copy in outs:
        copy.start()

    q = PW // 2

    def block(i, carry):
        rows = pl.ds(pl.multiple_of(i * q, q), q)
        gh, gl = [], []
        mine = jnp.logical_and(spread.row == spread.col, i < 2)
        for half in range(2):
            for s in range(4):
                for e in range(2):
                    value = G2[pl.ds((half * NB + i * q + e * BK) * 4 + s, BK, stride=4), :]
                    here = jnp.logical_and(jnp.logical_and(mine, spread.row == half), i % 2 * 2 + e == s)
                    value = value + jnp.where(here, on_diagonal(noise[s : s + 1, :]), 0.0)
                    hi, lo = split(value)
                    to = slice(half * PW + s * BK, half * PW + (s + 1) * BK)
                    Gh[e * BK : (e + 1) * BK, to] = hi
                    Gl[e * BK : (e + 1) * BK, to] = lo
        for j in range(4):
            to = pl.ds(j * q, q)
            kk = pl.ds(0, (j + 1) * q)
            E[rows, to] = dot3((Gh[:, kk], Gl[:, kk]), (Wh[to, kk], Wl[to, kk]), ((1,), (1,)))
        hi, lo = split(E[rows, :])
        Gh[...] = hi
        Gl[...] = lo
        for j in range(4):
            kk = pl.ds(j * q, NB - j * q)
            to = pl.ds(j * q, q)
            T[rows, to] = dot3((Gh[:, kk], Gl[:, kk]), (Wh[kk, to], Wl[kk, to]))
        return carry

    lax.fori_loop(0, 4, block, 0)
    outs.append(pltpu.make_async_copy(T, t_out, out_sem.at[2]))
    outs[2].start()
    outs.append(pltpu.make_async_copy(E.at[:, pl.ds(pl.multiple_of(spread.core * PW, PW), PW)], x_out, out_sem.at[3]))
    outs[3].start()
    for half in range(2):
        kh = [split(Tg[part]) for part in range(half + 1)]
        total = jnp.zeros((PW, BK), jnp.float32)
        for part in range(half + 1):
            kk = pl.ds(part * PW, PW)
            to = pl.ds(half * PW, PW)
            total = total + dot3((Wh[to, kk], Wl[to, kk]), kh[part])
        Hd[half] = total
    outs.append(pltpu.make_async_copy(Hd, head_out, out_sem.at[4]))
    outs[4].start()
    for copy in outs:
        copy.wait()


def front(cov, noise, tsrc):
    f32, bf16 = jnp.float32, jnp.bfloat16
    series = tsrc.shape[1]
    return pl.pallas_call(
        front_kernel,
        out_shape=(
            jax.ShapeDtypeStruct((NB, NB), f32),
            jax.ShapeDtypeStruct((NB, PW), f32),
            jax.ShapeDtypeStruct((2, PW, 4, 4, BK), f32),
            jax.ShapeDtypeStruct((2, PW, series), f32),
            jax.ShapeDtypeStruct((2, PW, series), f32),
        ),
        in_specs=[
            pl.BlockSpec(memory_space=pl.ANY),
            pl.BlockSpec(memory_space=pltpu.VMEM),
            pl.BlockSpec(memory_space=pl.ANY),
        ],
        out_specs=[pl.BlockSpec(memory_space=pl.ANY)] * 5,
        scratch_shapes=[
            pltpu.VMEM((2, PW, 4, 4, BK), f32),
            pltpu.VMEM((2, PW, series), f32),
            pltpu.VMEM((2, 2, PW, 4, BK), f32),
            pltpu.VMEM((3, PW, 4, BK), f32),
            pltpu.VMEM((NB, NB), f32),
            pltpu.VMEM((NB, NB), f32),
            pltpu.VMEM((BK, BK), f32),
            pltpu.VMEM((BK, NB), f32),
            pltpu.VMEM((NB, NB), bf16),
            pltpu.VMEM((NB, NB), bf16),
            pltpu.VMEM((PW // 2, NB), bf16),
            pltpu.VMEM((PW // 2, NB), bf16),
            pltpu.VMEM((NB, NB), bf16),
            pltpu.VMEM((NB, NB), bf16),
            pltpu.VMEM((2, PW, series), f32),
            pltpu.SemaphoreType.DMA((5,)),
        ]
        + spread_semaphores(),
        compiler_params=pltpu.CompilerParams(collective_id=0, has_side_effects=True, vmem_limit_bytes=56 * 2**20),
    )(cov, noise, tsrc)


UR = 256


def update_kernel(cov, noise, T, H, Tg, X, targets, head, out, reduced, Hh, Hl, Sh, Sl):
    step = pl.program_id(0)
    row, col = lax.axis_index("row"), lax.axis_index("col")

    @pl.when(step == 0)
    def _():
        def one(i, carry):
            rows = pl.ds(pl.multiple_of(i * BK, BK), BK)
            for s in range(16):
                to = slice(s * BK, (s + 1) * BK)
                Hh[rows, to], Hl[rows, to] = split(H[pl.ds(i * (BK * 16) + s, BK, stride=16), :])
            Sh[rows, :], Sl[rows, :] = split(Tg[rows, :])
            return carry

        lax.fori_loop(0, NB // BK, one, 0)

    lead = jnp.logical_and(row < 2, step < PW // UR)
    t0, t1 = split(T[:, 0:PW]), split(T[:, PW:NB])

    def minus(hi, lo, c0, n):
        to = pl.ds(c0, n)
        top, low = pl.ds(0, PW), pl.ds(PW, PW)
        return dot3(t0, (hi[top, to], lo[top, to])) + dot3(t1, (hi[low, to], lo[low, to]))

    i = lax.broadcasted_iota(jnp.int32, (UR, BK), 0) + (step // (PW // UR) * 16 + row) * PW + step % (PW // UR) * UR
    shifted = lax.broadcasted_iota(jnp.int32, (UR, BK), 0) - lax.broadcasted_iota(jnp.int32, (UR, BK), 1)
    for b in range(8):
        d = minus(Hh, Hl, b * 256, 256)
        for e in range(2):
            s = 2 * b + e
            on = jnp.logical_and(step // 2 * 16 + row == s // 4 * 8 + col, step % 2 == s % 4 // 2)
            line = jnp.where(on, noise[pl.ds(step // 2 * 4 + s % 4, 1), :], 0.0)
            value = cov[pl.ds(s, UR, stride=16), :] + jnp.where(shifted == s % 2 * BK, line, 0.0) - d[:, e * BK : (e + 1) * BK]
            value = jnp.where(lead, 0.0, value)
            if s < 4:
                j = lax.broadcasted_iota(jnp.int32, (UR, BK), 1) + col * PW + s * BK
                value = jnp.where(col < 2, jnp.where(i >= j, X[:, s * BK : (s + 1) * BK], 0.0), value)
            out[pl.ds(s, UR, stride=16), :] = value
    reduced[...] = jnp.where(lead, jnp.where(row == 0, head[0], head[1]), targets[...] - minus(Sh, Sl, 0, BK))


def update(cov, noise, T, H, Tg, X, targets, head):
    series = targets.shape[1]
    whole = lambda shape: pl.BlockSpec(shape, lambda i: (0,) * len(shape))
    rows = lambda n, m=1: pl.BlockSpec((UR * m, n), lambda i: (i, 0))
    bf16 = jnp.bfloat16
    return pl.pallas_call(
        update_kernel,
        grid=(NB // UR,),
        out_shape=(jax.ShapeDtypeStruct(cov.shape, jnp.float32), jax.ShapeDtypeStruct(targets.shape, jnp.float32)),
        in_specs=[
            rows(BK, 16),
            whole((8, BK)),
            rows(NB),
            whole((NB * 16, BK)),
            whole((NB, series)),
            rows(PW),
            rows(series),
            pl.BlockSpec((2, UR, series), lambda i: (0, i % (PW // UR), 0)),
        ],
        out_specs=[rows(BK, 16), rows(series)],
        scratch_shapes=[
            pltpu.VMEM((NB, 4 * PW), bf16),
            pltpu.VMEM((NB, 4 * PW), bf16),
            pltpu.VMEM((NB, series), bf16),
            pltpu.VMEM((NB, series), bf16),
        ],
        compiler_params=pltpu.CompilerParams(vmem_limit_bytes=56 * 2**20),
    )(cov, noise, T, H, Tg, X, targets, head)


def body(covariance, noise_var, observed, cloud_free):
    series = observed.shape[3]
    noise = noise_var.reshape(8, BK)
    targets = (observed * cloud_free.astype(jnp.float32)).reshape(NB, series)
    T, X, H, Tg, head = front(covariance.reshape(2, PW, 4, 4, BK), noise, targets[:PW])
    factor, reduced = update(
        covariance.reshape(NB * 16, BK), noise, T, H.reshape(NB * 16, BK), Tg.reshape(NB, series), X, targets, head
    )
    return factor.reshape(covariance.shape), reduced.reshape(observed.shape)


def solution(mesh):
    placed = (
        P(None, "row", None, None, "col", None),
        P(None, "row", None),
        P(None, "row", None, "col"),
        P(None, "row", None, "col"),
    )
    return jax.shard_map(
        body,
        mesh=mesh,
        in_specs=placed,
        out_specs=(P(None, "row", None, None, "col", None), P(None, "row", None, "col")),
        check_vma=False,
    )
```

```python
import jax
import jax.numpy as jnp
from jax import lax
from jax.experimental import pallas as pl
from jax.experimental.pallas import tpu as pltpu
from jax.sharding import PartitionSpec as P

MESH = pl.DeviceIdType.MESH
PW = 512
NB = 2 * PW
BK = 128
CH = 32
GC = 64

TREES = (
    (1, 11, 9, 0, 0, 7, 1, 0, 0, 4, 1, 0, 0, 4, 9, 0),
    (2, 0, 0, 0, 7, 8, 8, 14, 3, 3, 2, 2, 0, 0, 0, 0),
    (4, 0, 6, 14, 0, 0, 6, 1, 0, 0, 4, 1, 0, 0, 4, 13),
    (8, 0, 0, 0, 0, 0, 0, 0, 12, 8, 8, 12, 13, 11, 2, 2),
)


def tree_table():
    step = ((0, 1), (1, 0), (0, -1), (-1, 0))
    table = []
    for tree in TREES:
        depth = {0: 0}
        stack = [0]
        while stack:
            at = stack.pop()
            for d in range(4):
                if tree[at] >> d & 1:
                    to = (at // 4 + step[d][0]) % 4 * 4 + (at % 4 + step[d][1]) % 4
                    depth[to] = depth[at] + 1
                    stack.append(to)
        table.append([tree[at] | depth[at] << 4 for at in range(16)])
    return table


class Spread:
    LATE = (0, 1)
    GLATE = 8

    def __init__(self, cov, noise, tsrc, H, Tg, G, K, own, hr, hs, tr, ts, kr, ks, gr, gs):
        self.cov, self.noise, self.tsrc, self.own = cov, noise, tsrc, own
        self.H, self.Tg, self.G, self.K = H, Tg, G, K
        self.hr, self.hs, self.tr, self.ts = hr, hs, tr, ts
        self.kr, self.ks, self.gr, self.gs = kr, ks, gr, gs
        row, col = lax.axis_index("row"), lax.axis_index("col")
        y, z, x, core = row // 4, row % 4, col // 2, col % 2
        self.row, self.col, self.x, self.core = row, col, x, core
        self.where = [
            (y * 4 + (z + 1) % 4, col),
            (((y + 1) % 4) * 4 + z, col),
            (y * 4 + (z + 3) % 4, col),
            (((y + 3) % 4) * 4 + z, col),
            (row, ((x + 1) % 4) * 2 + core),
            (row, ((x + 3) % 4) * 2 + core),
            (row, x * 2 + 1 - core),
        ]
        self.mask, self.depth = [], []
        for root in range(2):
            place = y * 4 + (z + 4 - root) % 4
            masks, depths = [], []
            for entries in tree_table():
                v = jnp.int32(0)
                for at, entry in enumerate(entries):
                    v = jnp.where(place == at, entry, v)
                masks.append(v & 15)
                depths.append(v >> 4)
            self.mask.append(masks)
            self.depth.append(depths)
        self.hops = [x, (4 - x) % 4]
        self.on = [x != 3, x != 1]

    def remote(self, src, dst, send, recv, to):
        return pltpu.make_async_remote_copy(
            src_ref=src, dst_ref=dst, send_sem=send, recv_sem=recv, device_id=self.where[to], device_id_type=MESH
        )

    def hpiece(self, root, tree, n):
        at = pl.multiple_of((n % 4) * BK + tree * CH, CH)
        return self.H.at[root, pl.ds(at, CH), n // 4]

    def kpiece(self, block, tree, n):
        return self.K.at[block, pl.ds(pl.multiple_of(n * BK + tree * CH, CH), CH)]

    def gpiece(self, half, g):
        return self.G.at[half, g // 8, pl.ds(pl.multiple_of(g % 8 * GC, GC), GC)]

    def start(self):
        barrier = pltpu.get_barrier_semaphore()
        for device in self.where:
            pl.semaphore_signal(barrier, inc=1, device_id=device, device_id_type=MESH)
        for root in range(2):
            corner = pltpu.make_async_copy(self.cov.at[0, :, 0], self.H.at[root, :, 0], self.own)

            @pl.when(self.row == root)
            def _():
                corner.start()

                def own(n, carry):
                    for tree in range(4):
                        at = pl.multiple_of((n % 4) * BK + tree * CH, CH)
                        pltpu.make_async_copy(
                            self.cov.at[0, pl.ds(at, CH), n // 4],
                            self.hpiece(root, tree, n),
                            self.hr.at[root, tree, n],
                        ).start()
                    return carry

                lax.fori_loop(4, 16, own, 0)
                for tree in range(4):
                    rows = pl.ds(tree * BK, BK)
                    pltpu.make_async_copy(
                        self.tsrc.at[rows, :], self.Tg.at[root, rows, :], self.tr.at[root, tree]
                    ).start()
                corner.wait()

            @pl.when(jnp.logical_and(self.row == root, self.col == root))
            def _():
                for s in range(4):
                    rows = pl.ds(s * BK, BK)
                    self.H[root, rows, 0, s, :] = self.H[root, rows, 0, s, :] + on_diagonal(self.noise[s : s + 1, :])

        for half in range(2):

            @pl.when(self.col == half)
            def _():
                def own(g, carry):
                    pltpu.make_async_copy(
                        self.cov.at[g // 8, pl.ds(pl.multiple_of(g % 8 * GC, GC), GC), 0],
                        self.gpiece(half, g),
                        self.gr.at[half, g],
                    ).start()
                    return carry

                lax.fori_loop(0, 16, own, 0)
        pl.semaphore_wait(barrier, len(self.where))

    def slot(self, s):
        for root in range(2):
            for tree in range(4):
                depth, late = self.depth[root][tree], s - self.LATE[root]
                self.h_slot(root, tree, jnp.where(late - depth < 4, late - depth, jnp.where(late - 3 * depth < 4, -1, late - 3 * depth)))
        for block in range(3):
            for tree in range(4):
                root, way = block // 2, tree % 2
                n = s - self.LATE[root] - self.depth[root][tree] - self.hops[way]
                here = jnp.logical_and(self.core == min(block, 1), self.x != 0)

                @pl.when(jnp.logical_and(here, jnp.logical_and(n >= 0, n < 4)))
                def _():
                    piece, recv = self.kpiece(block, tree, n), self.kr.at[block, tree, n]
                    self.remote(piece, piece, self.ks.at[block, tree, 0], recv, 6).wait_recv()

                    @pl.when(self.on[way])
                    def _():
                        self.remote(piece, piece, self.ks.at[block, tree, 0], recv, 4 + way).start()

                    self.remote(piece, piece, self.ks.at[block, tree, 1], recv, 6).start()

        for half in range(2):
            for way in range(2):
                t = s - self.GLATE - 2 * self.hops[way]
                g = (t // 2) * 2 + way
                valid = jnp.logical_and(jnp.logical_and(t >= 0, t < 16), t % 2 == 0)

                @pl.when(jnp.logical_and(valid, self.core == half))
                def _():
                    piece, recv = self.gpiece(half, g), self.gr.at[half, g]
                    self.remote(piece, piece, self.gs.at[half, way, 0], recv, 6).wait_recv()

                    @pl.when(self.on[way])
                    def _():
                        self.remote(piece, piece, self.gs.at[half, way, 0], recv, 4 + way).start()

                    self.remote(piece, piece, self.gs.at[half, way, 1], recv, 6).start()

    def dirs(self, tree):
        return [d for d in range(4) if any(bits >> d & 1 for bits in TREES[tree])]

    def has(self, root, tree, d):
        return (self.mask[root][tree] >> d) & 1 == 1

    def h_slot(self, root, tree, n):
        @pl.when(jnp.logical_and(n >= 0, n < 16))
        def _():
            piece, recv = self.hpiece(root, tree, n), self.hr.at[root, tree, n]

            @pl.when(jnp.logical_or(self.row != root, n >= 4))
            def _():
                self.remote(piece, piece, self.hs.at[root, tree, 0], recv, 0).wait_recv()

            for d in self.dirs(tree):

                @pl.when(self.has(root, tree, d))
                def _():
                    self.remote(piece, piece, self.hs.at[root, tree, d], recv, d).start()

            for core in range(2):
                block = root + core
                if (root, core) == (1, 0):
                    continue

                @pl.when(jnp.logical_and(self.col == core, n < 4))
                def _():
                    m = jnp.minimum(n, 3)
                    to, krecv = self.kpiece(block, tree, m), self.kr.at[block, tree, m]
                    pltpu.make_async_copy(piece, to, krecv).start()
                    self.remote(piece, to, self.ks.at[block, tree, 0], krecv, 4 + tree % 2).start()
                    self.remote(piece, to, self.ks.at[block, tree, 1], krecv, 6).start()

        @pl.when(n == 16)
        def _():
            piece, recv = self.Tg.at[root, pl.ds(tree * BK, BK), :], self.tr.at[root, tree]
            self.remote(piece, piece, self.ts.at[root, tree, 0], recv, 0).wait_recv()
            for d in self.dirs(tree):

                @pl.when(self.has(root, tree, d))
                def _():
                    self.remote(piece, piece, self.ts.at[root, tree, d], recv, d).start()

    def corner_rows(self, block, n):
        @pl.when(jnp.logical_or(self.core != min(block, 1), self.x == 0))
        def _():
            for tree in range(4):
                piece, recv = self.kpiece(block, tree, n), self.kr.at[block, tree, n]
                self.remote(piece, piece, self.ks.at[block, tree, 0], recv, 6).wait_recv()

    def finish(self):
        for half in range(2):

            @pl.when(self.core != half)
            def _():
                def one(g, carry):
                    piece, recv = self.gpiece(half, g), self.gr.at[half, g]
                    self.remote(piece, piece, self.gs.at[half, 0, 0], recv, 6).wait_recv()
                    return carry

                lax.fori_loop(0, 16, one, 0)

            @pl.when(self.core == half)
            def _():
                for way in range(2):
                    whole = self.G.at[half, 0]
                    wait_sent(self, whole, self.gs.at[half, way, 1])

                    @pl.when(self.on[way])
                    def _():
                        wait_sent(self, whole, self.gs.at[half, way, 0])

        for root in range(2):
            for tree in range(4):
                for d in self.dirs(tree):

                    @pl.when(self.has(root, tree, d))
                    def _():
                        wait_sent(self, self.H.at[root, :, 0], self.hs.at[root, tree, d])
                        wait_sent(self, self.Tg.at[root, pl.ds(tree * BK, BK), :], self.ts.at[root, tree, d])

        for block in range(3):

            @pl.when(self.core == min(block, 1))
            def _():
                for tree in range(4):
                    whole = self.K.at[block, pl.ds(0, BK)]
                    wait_sent(self, whole, self.ks.at[block, tree, 1])

                    @pl.when(self.on[tree % 2])
                    def _():
                        wait_sent(self, whole, self.ks.at[block, tree, 0])


def on_diagonal(line):
    i = lax.broadcasted_iota(jnp.int32, (BK, BK), 0)
    j = lax.broadcasted_iota(jnp.int32, (BK, BK), 1)
    return jnp.where(i == j, line, 0.0)


def wait_sent(spread, whole, sem):
    spread.remote(whole, whole, sem, spread.gr.at[0, 0], 6).wait_send()


def spread_semaphores():
    dma = pltpu.SemaphoreType.DMA
    return [
        dma,
        dma((2, 4, 16)),
        dma((2, 4, 4)),
        dma((2, 4)),
        dma((2, 4, 4)),
        dma((3, 4, 4)),
        dma((3, 4, 2)),
        dma((2, 16)),
        dma((2, 2, 2)),
    ]


def factor128(read, halfway):
    lane = lax.broadcasted_iota(jnp.int32, (8, BK), 1)
    sub = lax.broadcasted_iota(jnp.int32, (8, BK), 0)
    R = [read(p) for p in range(16)]
    Q = [jnp.where(lane == sub + 8 * p, 1.0, 0.0) for p in range(16)]
    splat = lambda v: jnp.broadcast_to(v, (8, BK))
    W = []
    for p in range(16):
        if p == 8:
            halfway()
        B = [splat(R[p][:, 8 * p + k : 8 * p + k + 1]) for k in range(8)]
        below = {i: [splat(R[i][:, 8 * p + k : 8 * p + k + 1]) for k in range(8)] for i in range(p + 1, 16)}
        Rp, Qp = R[p], Q[p]
        pivots = None
        for j in range(8):
            d = splat(B[j][j : j + 1, :])
            inv = pltpu.reciprocal(d, approx=True)
            pivots = d if pivots is None else jnp.where(sub == j, d, pivots)
            coef = jnp.where(sub > j, B[j] * inv, 0.0)
            ur, qr = splat(Rp[j : j + 1, :]), splat(Qp[j : j + 1, :])
            lead = {k: splat(B[k][j : j + 1, :]) for k in range(j + 1, 8)}
            for i in range(p + 1, 16):
                ci = below[i][j] * inv
                for k in range(j + 1, 8):
                    below[i][k] = below[i][k] - ci * lead[k]
                R[i] = R[i] - ci * ur
                Q[i] = Q[i] - ci * qr
            if j < 7:
                for k in range(j + 1, 8):
                    B[k] = B[k] - coef * lead[k]
                Rp = Rp - coef * ur
                Qp = Qp - coef * qr
        scale = lax.rsqrt(pivots)
        W.append(Qp * scale)
    return W


def split(v):
    hi = v.astype(jnp.bfloat16)
    return hi, (v - hi.astype(jnp.float32)).astype(jnp.bfloat16)


def dot3(a, b, dims=((1,), (0,))):
    one = lambda u, v: lax.dot_general(u, v, (dims, ((), ())), preferred_element_type=jnp.float32)
    return one(a[0], b[0]) + (one(a[0], b[1]) + one(a[1], b[0]))


def less_above(k, line, Uh, Ul, Wh, Wl):
    for c in range(1, NB // BK):

        @pl.when(k == c)
        def _():
            top, here = pl.ds(0, c * BK), pl.ds(c * BK, BK)
            u = (Uh[top, here], Ul[top, here])
            for first in range(0, NB, 2 * BK):
                for hi, lo, start, stop in ((Wh, Wl, 0, c * BK), (Uh, Ul, c * BK, NB)):
                    start, stop = max(first, start), min(first + 2 * BK, stop)
                    if start < stop:
                        to = pl.ds(start, stop - start)
                        line[:, to] = line[:, to] - dot3(u, (hi[top, to], lo[top, to]), ((0,), (0,)))


def finish_row(r0, inverse, line, Uh, Ul, Wh, Wl):
    rows = pl.ds(r0, BK)
    whole = dot3(split(inverse[...]), split(line[...]))
    lane = lax.broadcasted_iota(jnp.int32, (BK, NB), 1)
    Uh[rows, :], Ul[rows, :] = split(jnp.where(lane >= r0 + BK, whole, 0.0))
    Wh[rows, :], Wl[rows, :] = split(jnp.where(lane < r0, whole, 0.0))
    Wh[rows, pl.ds(r0, BK)], Wl[rows, pl.ds(r0, BK)] = split(inverse[...])


PRE = 9
PER = 3


def front_kernel(cov, noise, tsrc, t_out, x_out, h_out, g_out, head_out, H, Tg, G, K, E, T, D, line, Uh, Ul, Gh, Gl, Wh, Wl, Hd, out_sem, *sems):
    spread = Spread(cov, noise, tsrc, H, Tg, G, K, *sems)
    count = NB // BK

    def slots(first, n):
        def one(s, carry):
            spread.slot(s)
            return carry

        lax.fori_loop(first, first + n, one, 0)

    K2, G2 = K.reshape(3 * PW * 4, BK), G.reshape(2 * NB * 4, BK)
    spread.start()
    slots(0, PRE)
    lane = lax.broadcasted_iota(jnp.int32, (BK, BK), 1)

    def step(k, carry):
        r0 = pl.multiple_of(k * BK, BK)
        spread.slot(PRE + PER * k)

        @pl.when(k < 4)
        def _():
            n = jnp.minimum(k, 3)
            spread.corner_rows(0, n)
            spread.corner_rows(1, n)
            for s in range(4):
                value = K2[pl.ds(n * (BK * 4) + s, BK, stride=4), :]
                line[:, s * BK : (s + 1) * BK] = jnp.where(lane + s * BK >= r0, value, 0.0)
                line[:, PW + s * BK : PW + (s + 1) * BK] = K2[pl.ds((PW + n * BK) * 4 + s, BK, stride=4), :]

        @pl.when(k >= 4)
        def _():
            n = jnp.maximum(k - 4, 0)
            spread.corner_rows(2, n)
            for s in range(4):
                value = K2[pl.ds((2 * PW + n * BK) * 4 + s, BK, stride=4), :]
                line[:, s * BK : (s + 1) * BK] = jnp.zeros((BK, BK), jnp.float32)
                line[:, PW + s * BK : PW + (s + 1) * BK] = jnp.where(lane + PW + s * BK >= r0, value, 0.0)

        less_above(k, line, Uh, Ul, Wh, Wl)
        W = factor128(lambda p: line[8 * p : 8 * p + 8, pl.ds(r0, BK)], lambda: spread.slot(PRE + PER * k + 1))
        for p in range(16):
            D[pl.ds(8 * p, 8), :] = W[p]
        spread.slot(PRE + PER * k + 2)
        finish_row(r0, D, line, Uh, Ul, Wh, Wl)
        return carry

    lax.fori_loop(0, count, step, 0)
    spread.finish()
    outs = [pltpu.make_async_copy(H, h_out, out_sem.at[0]), pltpu.make_async_copy(Tg, g_out, out_sem.at[1])]
    for copy in outs:
        copy.start()

    q = PW // 2

    def block(i, carry):
        rows = pl.ds(pl.multiple_of(i * q, q), q)
        gh, gl = [], []
        mine = jnp.logical_and(spread.row == spread.col, i < 2)
        for half in range(2):
            for s in range(4):
                for e in range(2):
                    value = G2[pl.ds((half * NB + i * q + e * BK) * 4 + s, BK, stride=4), :]
                    here = jnp.logical_and(jnp.logical_and(mine, spread.row == half), i % 2 * 2 + e == s)
                    value = value + jnp.where(here, on_diagonal(noise[s : s + 1, :]), 0.0)
                    hi, lo = split(value)
                    to = slice(half * PW + s * BK, half * PW + (s + 1) * BK)
                    Gh[e * BK : (e + 1) * BK, to] = hi
                    Gl[e * BK : (e + 1) * BK, to] = lo
        for j in range(4):
            to = pl.ds(j * q, q)
            kk = pl.ds(0, (j + 1) * q)
            E[rows, to] = dot3((Gh[:, kk], Gl[:, kk]), (Wh[to, kk], Wl[to, kk]), ((1,), (1,)))
        hi, lo = split(E[rows, :])
        Gh[...] = hi
        Gl[...] = lo
        for j in range(4):
            kk = pl.ds(j * q, NB - j * q)
            to = pl.ds(j * q, q)
            T[rows, to] = dot3((Gh[:, kk], Gl[:, kk]), (Wh[kk, to], Wl[kk, to]))
        return carry

    lax.fori_loop(0, 4, block, 0)
    outs.append(pltpu.make_async_copy(T, t_out, out_sem.at[2]))
    outs[2].start()
    outs.append(pltpu.make_async_copy(E.at[:, pl.ds(pl.multiple_of(spread.core * PW, PW), PW)], x_out, out_sem.at[3]))
    outs[3].start()
    for half in range(2):
        kh = [split(Tg[part]) for part in range(half + 1)]
        total = jnp.zeros((PW, BK), jnp.float32)
        for part in range(half + 1):
            kk = pl.ds(part * PW, PW)
            to = pl.ds(half * PW, PW)
            total = total + dot3((Wh[to, kk], Wl[to, kk]), kh[part])
        Hd[half] = total
    outs.append(pltpu.make_async_copy(Hd, head_out, out_sem.at[4]))
    outs[4].start()
    for copy in outs:
        copy.wait()


def front(cov, noise, tsrc):
    f32, bf16 = jnp.float32, jnp.bfloat16
    series = tsrc.shape[1]
    return pl.pallas_call(
        front_kernel,
        out_shape=(
            jax.ShapeDtypeStruct((NB, NB), f32),
            jax.ShapeDtypeStruct((NB, PW), f32),
            jax.ShapeDtypeStruct((2, PW, 4, 4, BK), f32),
            jax.ShapeDtypeStruct((2, PW, series), f32),
            jax.ShapeDtypeStruct((2, PW, series), f32),
        ),
        in_specs=[
            pl.BlockSpec(memory_space=pl.ANY),
            pl.BlockSpec(memory_space=pltpu.VMEM),
            pl.BlockSpec(memory_space=pl.ANY),
        ],
        out_specs=[pl.BlockSpec(memory_space=pl.ANY)] * 5,
        scratch_shapes=[
            pltpu.VMEM((2, PW, 4, 4, BK), f32),
            pltpu.VMEM((2, PW, series), f32),
            pltpu.VMEM((2, 2, PW, 4, BK), f32),
            pltpu.VMEM((3, PW, 4, BK), f32),
            pltpu.VMEM((NB, NB), f32),
            pltpu.VMEM((NB, NB), f32),
            pltpu.VMEM((BK, BK), f32),
            pltpu.VMEM((BK, NB), f32),
            pltpu.VMEM((NB, NB), bf16),
            pltpu.VMEM((NB, NB), bf16),
            pltpu.VMEM((PW // 2, NB), bf16),
            pltpu.VMEM((PW // 2, NB), bf16),
            pltpu.VMEM((NB, NB), bf16),
            pltpu.VMEM((NB, NB), bf16),
            pltpu.VMEM((2, PW, series), f32),
            pltpu.SemaphoreType.DMA((5,)),
        ]
        + spread_semaphores(),
        compiler_params=pltpu.CompilerParams(collective_id=0, has_side_effects=True, vmem_limit_bytes=56 * 2**20),
    )(cov, noise, tsrc)


UR = 256


def update_kernel(cov, noise, T, H, Tg, X, targets, head, out, reduced, Hh, Hl, Sh, Sl):
    step = pl.program_id(0)
    row, col = lax.axis_index("row"), lax.axis_index("col")

    @pl.when(step == 0)
    def _():
        def one(i, carry):
            rows = pl.ds(pl.multiple_of(i * BK, BK), BK)
            for s in range(16):
                to = slice(s * BK, (s + 1) * BK)
                Hh[rows, to], Hl[rows, to] = split(H[pl.ds(i * (BK * 16) + s, BK, stride=16), :])
            Sh[rows, :], Sl[rows, :] = split(Tg[rows, :])
            return carry

        lax.fori_loop(0, NB // BK, one, 0)

    lead = jnp.logical_and(row < 2, step < PW // UR)
    t0, t1 = split(T[:, 0:PW]), split(T[:, PW:NB])

    def minus(hi, lo, c0, n):
        to = pl.ds(c0, n)
        top, low = pl.ds(0, PW), pl.ds(PW, PW)
        return dot3(t0, (hi[top, to], lo[top, to])) + dot3(t1, (hi[low, to], lo[low, to]))

    i = lax.broadcasted_iota(jnp.int32, (UR, BK), 0) + (step // (PW // UR) * 16 + row) * PW + step % (PW // UR) * UR
    shifted = lax.broadcasted_iota(jnp.int32, (UR, BK), 0) - lax.broadcasted_iota(jnp.int32, (UR, BK), 1)
    for b in range(8):
        d = minus(Hh, Hl, b * 256, 256)
        for e in range(2):
            s = 2 * b + e
            on = jnp.logical_and(step // 2 * 16 + row == s // 4 * 8 + col, step % 2 == s % 4 // 2)
            line = jnp.where(on, noise[pl.ds(step // 2 * 4 + s % 4, 1), :], 0.0)
            value = cov[pl.ds(s, UR, stride=16), :] + jnp.where(shifted == s % 2 * BK, line, 0.0) - d[:, e * BK : (e + 1) * BK]
            value = jnp.where(lead, 0.0, value)
            if s < 4:
                j = lax.broadcasted_iota(jnp.int32, (UR, BK), 1) + col * PW + s * BK
                value = jnp.where(col < 2, jnp.where(i >= j, X[:, s * BK : (s + 1) * BK], 0.0), value)
            out[pl.ds(s, UR, stride=16), :] = value
    reduced[...] = jnp.where(lead, jnp.where(row == 0, head[0], head[1]), targets[...] - minus(Sh, Sl, 0, BK))


def update(cov, noise, T, H, Tg, X, targets, head):
    series = targets.shape[1]
    whole = lambda shape: pl.BlockSpec(shape, lambda i: (0,) * len(shape))
    rows = lambda n, m=1: pl.BlockSpec((UR * m, n), lambda i: (i, 0))
    bf16 = jnp.bfloat16
    return pl.pallas_call(
        update_kernel,
        grid=(NB // UR,),
        out_shape=(jax.ShapeDtypeStruct(cov.shape, jnp.float32), jax.ShapeDtypeStruct(targets.shape, jnp.float32)),
        in_specs=[
            rows(BK, 16),
            whole((8, BK)),
            rows(NB),
            whole((NB * 16, BK)),
            whole((NB, series)),
            rows(PW),
            rows(series),
            pl.BlockSpec((2, UR, series), lambda i: (0, i % (PW // UR), 0)),
        ],
        out_specs=[rows(BK, 16), rows(series)],
        scratch_shapes=[
            pltpu.VMEM((NB, 4 * PW), bf16),
            pltpu.VMEM((NB, 4 * PW), bf16),
            pltpu.VMEM((NB, series), bf16),
            pltpu.VMEM((NB, series), bf16),
        ],
        compiler_params=pltpu.CompilerParams(vmem_limit_bytes=56 * 2**20),
    )(cov, noise, T, H, Tg, X, targets, head)


def body(covariance, noise_var, observed, cloud_free):
    series = observed.shape[3]
    noise = noise_var.reshape(8, BK)
    targets = (observed * cloud_free.astype(jnp.float32)).reshape(NB, series)
    T, X, H, Tg, head = front(covariance.reshape(2, PW, 4, 4, BK), noise, targets[:PW])
    factor, reduced = update(
        covariance.reshape(NB * 16, BK), noise, T, H.reshape(NB * 16, BK), Tg.reshape(NB, series), X, targets, head
    )
    return factor.reshape(covariance.shape), reduced.reshape(observed.shape)


def solution(mesh):
    placed = (
        P(None, "row", None, None, "col", None),
        P(None, "row", None),
        P(None, "row", None, "col"),
        P(None, "row", None, "col"),
    )
    return jax.shard_map(
        body,
        mesh=mesh,
        in_specs=placed,
        out_specs=(P(None, "row", None, None, "col", None), P(None, "row", None, "col")),
        check_vma=False,
    )
```
